32 devices in a mesh: groups: 2 (over y), expert: 4 (over x, core), replica: 4 (over z).
Axes of the slice: x: 2, y: 2, z: 4, core: 2. Of those that a mesh axis runs over, the one named last changes fastest.
Arguments:
- grad_rows: bfloat16 [4096, 3584], P(('groups', 'expert', 'replica')), parts along dimension 0, may hold values from -6 to 6
- grad_scale: float32 [4096], P(('groups', 'expert', 'replica')), parts along dimension 0, may hold values from 0.25 to 4
- route_probs: float32 [4096, 8], P(('groups', 'expert', 'replica')), parts along dimension 0, may hold values from 0.1 to 0.6
- expert_ids: int32 [4096, 8], P(('groups', 'expert', 'replica')), parts along dimension 0, may hold values from 0 to 15, all different within a row; in each aligned block of 128 rows (0 to 127, 128 to 255, ...) at most 72 rows name the same one
- saved_hidden: bfloat16 [8, 16, 4, 72, 1024], P(('groups', 'replica'), 'expert'), parts along dimension 0, may hold values from -6 to 6
Outputs:
- weight_grad: bfloat16 [2048, 16, 3584], P(('groups', 'replica'), 'expert'), parts along dimension 0
The draws below stay inside these ranges and needn't reach their ends.
There are 2 independent parts, one for each index of `groups`. The reference program is written for one: setup_inputs(seed, part) draws one part's arguments, and reference() takes and returns one part's arrays. A program takes and returns all parts, laid end to end along the dimension named above; each array names one. Nothing has to cross between parts.
Inputs may be any that keep to these rules, and one draw needn't show every extreme that they name: `expert_ids`: each token names 8 different experts. The 128 tokens of one device name one expert at most 72 times, and in every draw some device names some expert exactly 72 times.
All inputs are finite; a program needn't handle non-finite values.
Results may differ from the reference program's by a relative error of at most 0.0095.
Values may be sent and summed in bfloat16 or wider, within the bound.
No kernel may reach another device: no remote copies, remote signals or barrier semaphores. Data moves between devices by JAX's collectives and lax.ppermute only.
A program may use at most 128 MiB of HBM per device.

```python
import math
import jax
import jax.numpy as jnp
import numpy as np
from jax import lax

D = 3584
FW = 1024
EXPERTS = 16
TOPK = 8
TOK_DEV = 128
CAP = 72
TOKENS = 2048
N_EXPERT = 4
N_REPLICA = 4


def spiked(result, key, source, target, shards_of, factor):
    owner, partner = [(jnp.arange(result.shape[axis_at]) // (result.shape[axis_at] // shards_of)).reshape([-1 if axis == axis_at else 1 for axis in range(result.ndim)]) for axis_at in (source, target)]
    chosen = jax.random.permutation(key, shards_of)[partner]
    strong = (owner == chosen) | (owner == (partner + shards_of // 2) % shards_of)
    return jnp.where(strong, factor * result, result)


def levels(key, extent, split, smallest, top_value):
    gain = 1.0
    for dim, blocks in split:
        steps = jax.random.uniform(jax.random.fold_in(jax.random.fold_in(key, 6), dim), (blocks,), jnp.float32, smallest / len(split), top_value / len(split))
        gain = gain * jnp.repeat(jnp.exp(steps), extent[dim] // blocks).reshape((-1,) + (1,) * (len(extent) - 1 - dim))
    return gain


def deal_out(stream_key, own, number, rows, number_of, top, limit, lean):
    sequence = jax.random.permutation(stream_key, number_of)
    crowded, usual = portions_of(number_of, rows * top, limit, lean, True), portions_of(number_of, rows * top, limit, lean, False)
    places = jnp.arange(number_of)

    def named(lengths, rotation):
        used = int((lengths > 0).sum())
        fixed = max(1, used // 4)
        shifted = fixed + (places - fixed + rotation * (used - fixed)) % max(1, number_of - fixed)
        return jnp.zeros((number_of,), jnp.int32).at[sequence[jnp.where(places < fixed, places, shifted)]].set(jnp.asarray(lengths, jnp.int32))

    lengths = jnp.where(number % 4 == 0, named(crowded, number // 4), named(usual, number - number // 4 - 1))
    mixed = jax.random.permutation(jax.random.fold_in(own, 3), number_of)
    donor, sink = mixed[0:number_of // 2 * 2:2], mixed[1:number_of // 2 * 2:2]
    margin = jnp.minimum(lengths[donor] - 1, limit - lengths[sink]) // 2
    margin = jnp.where((donor == sequence[0]) | (sink == sequence[0]) | (lengths[sink] == 0), 0, jnp.maximum(margin, 0))
    shifted = jax.random.randint(jax.random.fold_in(own, 4), (number_of // 2,), 0, 1 << 20) % (margin + 1)
    lengths = lengths.at[donor].add(-shifted).at[sink].add(shifted)
    items = jnp.searchsorted(jnp.cumsum(lengths), jnp.arange(rows * top), side="right").astype(jnp.int32)
    listing = items.reshape(top, rows).T
    listing = listing[jax.random.permutation(jax.random.fold_in(own, 1), rows)]
    rotation = jax.random.randint(jax.random.fold_in(own, 2), (rows, 1), 0, top)
    return jnp.take_along_axis(listing, (jnp.arange(top)[None, :] + rotation) % top, axis=1)


def portions_of(count, total, reach, slope, full):
    weights = [(1 << 20) // math.isqrt(grade ** slope) + 1 for grade in range(1, count + 1)]
    largest = reach if full else min(reach, max(-(-total // count), total * weights[0] // sum(weights)))
    least = 1 if total - largest >= count - 1 else 0
    given, surplus = [largest] + [least] * (count - 1), total - largest - least * (count - 1)
    while surplus > 0:
        movable = [i for i in range(1, count) if given[i] < largest] or [i for i in range(1, count) if given[i] < reach]
        pool, remaining = sum([weights[i] for i in movable]), surplus
        for i in movable:
            addition = min(reach - given[i], max(1, remaining * weights[i] // pool), surplus)
            given[i] = given[i] + addition
            surplus = surplus - addition
    return np.array(given)


def scatter_about(stream_key, dims, width, most, pieces=(), kind=jnp.bfloat16):
    loudness = levels(stream_key, dims, pieces, -0.22, 0.18) if pieces else 1.0
    array = jax.random.normal(stream_key, dims, jnp.float32) * width * loudness
    return jnp.minimum(jnp.maximum(array, -most), most).astype(kind)


def heavy_noise(rng, dims, width, bound, pieces, heavy, kind=jnp.bfloat16):
    entries = width * jax.random.normal(rng, dims, jnp.float32)
    if pieces:
        entries = entries * levels(rng, dims, pieces, -0.22, 0.18)
    return jnp.clip(spiked(entries, jax.random.fold_in(rng, 3), *heavy), -bound, bound).astype(kind)


def setup_inputs(seed: int = 0, part: int = 0) -> dict:
    key_of = jax.random.split(jax.random.key(seed), 6)
    part_splits = jax.random.split(jax.random.fold_in(key_of[5], part), 6)
    grad_rows = scatter_about(part_splits[0], (TOKENS, D), 1.0, 6.0, ((0, 16),))
    grad_scale = jnp.clip(jnp.exp(math.log(4.0) - 2.7725887 * jax.random.uniform(part_splits[1], (TOKENS,), jnp.float32) ** levels(part_splits[1], (TOKENS,), ((0, 16),), -0.2, 0.2)), 0.25, 4.0)
    route_probs = jnp.clip(0.1 + 0.5 * jax.random.uniform(part_splits[2], (TOKENS, TOPK), jnp.float32) ** levels(part_splits[2], (TOKENS, TOPK), ((0, 16),), -0.2, 0.2), 0.1, 0.6)
    expert_ids_keys = jax.random.split(jax.random.fold_in(part_splits[3], 1), TOKENS // TOK_DEV)
    expert_ids_turns = jax.random.permutation(jax.random.fold_in(part_splits[3], 3), TOKENS // TOK_DEV)
    expert_ids = jax.vmap(lambda own, number: deal_out(jax.random.fold_in(part_splits[3], 2), own, number, TOK_DEV, EXPERTS, TOPK, CAP, 2))(expert_ids_keys, expert_ids_turns).reshape((TOKENS, TOPK))
    saved_hidden = heavy_noise(part_splits[4], (N_REPLICA, EXPERTS, N_EXPERT, CAP, FW), 1.0, 6.0, ((0, 4), (1, 4)), (0, 4, 4, 2.0))
    return dict(grad_rows=grad_rows, grad_scale=grad_scale, route_probs=route_probs, expert_ids=expert_ids, saved_hidden=saved_hidden)


def reference(grad_rows, grad_scale, route_probs, expert_ids, saved_hidden):
    scale_norm = 1.0 / math.sqrt(N_REPLICA * N_EXPERT * TOK_DEV * TOPK / EXPERTS)
    token_rows = grad_rows.reshape(N_EXPERT, N_REPLICA, TOK_DEV, D)
    pair_coef = (grad_scale[:, None] * route_probs).reshape(N_EXPERT, N_REPLICA, TOK_DEV * TOPK)
    pair_ids = expert_ids.reshape(N_EXPERT, N_REPLICA, TOK_DEV * TOPK)
    onehot = (pair_ids[..., None] == jnp.arange(EXPERTS, dtype=jnp.int32)).astype(jnp.int32)
    position = lax.optimization_barrier(jnp.sum(onehot * jnp.cumsum(onehot, axis=2), axis=3)) - 1
    slot_index = (pair_ids * CAP + position).astype(jnp.int32)
    pair_token = jnp.arange(TOK_DEV * TOPK, dtype=jnp.int32) // TOPK

    def replica_sum(running, replica):

        def source_sum(partial_value, source):
            block_rows = token_rows[source, replica]
            scaled = (pair_coef[source, replica][:, None] * block_rows[pair_token]).astype(jnp.bfloat16)
            bucket = jnp.zeros((EXPERTS * CAP, D), jnp.bfloat16).at[slot_index[source, replica]].set(scaled)
            bucket = bucket.reshape(EXPERTS, CAP, D).astype(jnp.float32)
            hidden = saved_hidden[replica, :, source].astype(jnp.float32)
            return (partial_value + jnp.einsum('jcf,jcd->fjd', hidden, bucket), None)
        partial_value, _ = lax.scan(source_sum, jnp.zeros((FW, EXPERTS, D), jnp.float32), jnp.arange(N_EXPERT, dtype=jnp.int32))
        rounded = lax.optimization_barrier((partial_value * scale_norm).astype(jnp.bfloat16))
        return (running + rounded.astype(jnp.float32), None)
    total_sum, _ = lax.scan(replica_sum, jnp.zeros((FW, EXPERTS, D), jnp.float32), jnp.arange(N_REPLICA, dtype=jnp.int32))
    return total_sum.astype(jnp.bfloat16)
```

```python
import math

import jax
import jax.numpy as jnp
from jax import lax
from jax.experimental import pallas as pl
from jax.experimental.pallas import tpu as pltpu
from jax.sharding import PartitionSpec as P

EXPERTS = 16


def slot_positions(expert_ids):
    flat_ids = expert_ids.reshape(-1)
    onehot = (flat_ids[:, None] == jnp.arange(EXPERTS, dtype=jnp.int32)[None, :]).astype(jnp.int32)
    running = jnp.cumsum(onehot, axis=0)
    return (flat_ids, jnp.sum(onehot * running, axis=1) - 1)


def summed_shards(grad_rows, grad_scale, route_probs, expert_ids, saved_hidden):
    tok_rows, row_width = grad_rows.shape
    top_count = expert_ids.shape[1]
    n_expert = lax.axis_size("expert")
    n_replica = lax.axis_size("replica")
    per_device = EXPERTS // n_expert
    hidden = saved_hidden[0]
    capacity = hidden.shape[2]
    hidden_units = hidden.shape[3]
    scale_norm = 1.0 / math.sqrt(n_replica * n_expert * tok_rows * top_count / EXPERTS)
    flat_ids, position = slot_positions(expert_ids)
    pair_coef = grad_scale[:, None] * route_probs
    gathered_ids, gathered_pos = (
        lax.all_gather(expert_ids, "expert", axis=0, tiled=True),
        lax.all_gather(position.reshape(tok_rows, top_count), "expert", axis=0, tiled=True),
    )
    gathered_coef = lax.all_gather(pair_coef, "expert", axis=0, tiled=True)
    first_expert = lax.axis_index("expert") * per_device
    local_ids = first_expert + jnp.arange(per_device, dtype=jnp.int32)
    hidden_flat = hidden.reshape(per_device, n_expert * capacity, hidden_units)
    token_piece = lax.all_gather(grad_rows, "expert", axis=0, tiled=True)
    row_count = token_piece.shape[0]
    source = jnp.arange(row_count, dtype=jnp.int32) // tok_rows
    matches = gathered_ids[None, :, :] == local_ids[:, None, None]
    row_coef = jnp.sum(jnp.where(matches, gathered_coef[None], 0.0), axis=2)
    row_index = jnp.sum(
        jnp.where(matches, source[None, :, None] * capacity + gathered_pos[None], 0), axis=2
    )
    chosen = jax.vmap(lambda hidden_table, row_pick: jnp.take(hidden_table, row_pick, axis=0))(
        hidden_flat, row_index
    )
    scaled = (row_coef[:, :, None] * token_piece[None]).astype(jnp.bfloat16)
    summed = jnp.einsum("lif,lid->fld", chosen, scaled, preferred_element_type=jnp.float32)
    return lax.psum_scatter(
        (summed * scale_norm).astype(jnp.bfloat16), "replica", scatter_dimension=0, tiled=True
    )


def spread_kernel(where_ref, hidden_ref, meta_ref, out_ref, rows_ref):
    experts, sources, capacity, units = hidden_ref.shape
    tok = meta_ref.shape[2]
    me, replica = where_ref[0], where_ref[1]
    for q in range(sources):
        src = me ^ q
        block = src * sources + replica
        for j in range(experts):
            pos = meta_ref[block, pl.ds(j, 1), :]
            coef = meta_ref[block, pl.ds(experts + j, 1), :]
            slot = lax.broadcasted_iota(jnp.int32, (capacity, tok), 0).astype(jnp.float32)
            pick = jnp.where(slot == pos, 1.0, 0.0).astype(jnp.bfloat16)
            rows = lax.dot_general(
                hidden_ref[j, src],
                pick,
                (((0,), (0,)), ((), ())),
                preferred_element_type=jnp.float32,
            )
            rows_ref[pl.ds(j, units, stride=experts), :] = rows * coef
        out_ref[:, q * tok : (q + 1) * tok] = rows_ref[...].astype(out_ref.dtype)


def spread(where, hidden, meta):
    experts, sources, capacity, units = hidden.shape
    tok = meta.shape[2]
    vmem = pl.BlockSpec(memory_space=pltpu.VMEM)
    return pl.pallas_call(
        spread_kernel,
        out_shape=jax.ShapeDtypeStruct((units * experts, sources * tok), jnp.bfloat16),
        in_specs=[pl.BlockSpec(memory_space=pltpu.SMEM), vmem, vmem],
        out_specs=vmem,
        scratch_shapes=[pltpu.VMEM((units * experts, tok), jnp.float32)],
        compiler_params=pltpu.CompilerParams(vmem_limit_bytes=16 << 20),
        cost_estimate=pl.CostEstimate(
            flops=2 * sources * experts * units * tok * capacity * 2,
            bytes_accessed=hidden.size * 2 + units * experts * sources * tok * 2,
            transcendentals=0,
        ),
    )(where, hidden, meta)


def product(flag, spreads, rows, other=None, acc=None, last=False, experts=4, tile=512):
    n_tok, width = rows[0].shape
    m = spreads[0].shape[0]
    steps = width // tile
    sets = [rows] + ([other] if other is not None else [])

    def body(flag_ref, *refs):
        refs = list(refs)
        lhs = [refs.pop(0) for _ in spreads]
        held = [[refs.pop(0) for _ in group] for group in sets]
        before = refs.pop(0) if acc is not None else None
        out = refs.pop(0)
        k = jnp.concatenate([r[...] for r in held[0]], axis=0)
        if other is not None:
            k2 = jnp.concatenate([r[...] for r in held[1]], axis=0)
            k = jnp.where(flag_ref[0] == 1, k, k2)
        left = jnp.concatenate([r[...] for r in lhs], axis=1) if len(lhs) > 1 else lhs[0][...]
        total = jnp.dot(left, k, preferred_element_type=jnp.float32)
        if before is not None:
            total = total + before[...]
        if last:
            out[...] = total.reshape(m // experts, experts, tile).astype(out.dtype)
        else:
            out[...] = total

    in_specs = [pl.BlockSpec(s.shape, lambda i, f: (0, 0)) for s in spreads]
    for n, group in enumerate(sets):
        if other is None:
            pick = lambda i, f: (0, i)
        elif n == 0:
            pick = lambda i, f: (0, i * f[0])
        else:
            pick = lambda i, f: (0, i * (1 - f[0]))
        in_specs += [pl.BlockSpec((n_tok, tile), pick) for _ in group]
    args = list(spreads) + [r for group in sets for r in group]
    aliases = {}
    if acc is not None:
        in_specs.append(pl.BlockSpec((m, tile), lambda i, f: (0, i)))
        if not last:
            aliases = {1 + len(args): 0}
        args.append(acc)
    if last:
        out_shape = jax.ShapeDtypeStruct((m // experts, experts, width), jnp.bfloat16)
        out_spec = pl.BlockSpec((m // experts, experts, tile), lambda i, f: (0, 0, i))
    else:
        out_shape = jax.ShapeDtypeStruct((m, width), jnp.float32)
        out_spec = pl.BlockSpec((m, tile), lambda i, f: (0, i))
    k = sum(s.shape[1] for s in spreads)
    return pl.pallas_call(
        body,
        grid_spec=pltpu.PrefetchScalarGridSpec(
            num_scalar_prefetch=1, grid=(steps,), in_specs=in_specs, out_specs=out_spec
        ),
        out_shape=out_shape,
        input_output_aliases=aliases,
        compiler_params=pltpu.CompilerParams(vmem_limit_bytes=40 << 20),
        cost_estimate=pl.CostEstimate(
            flops=2 * m * k * width,
            bytes_accessed=m * width * 4 + k * width * 2,
            transcendentals=0,
        ),
    )(flag, *args)


def gathered_shards(grad_rows, grad_scale, route_probs, expert_ids, saved_hidden):
    tok, width = grad_rows.shape
    top_count = expert_ids.shape[1]
    n_expert = lax.axis_size("expert")
    n_replica = lax.axis_size("replica")
    per_device = EXPERTS // n_expert
    hidden = saved_hidden[0]
    units = hidden.shape[3] // n_replica
    scale_norm = 1.0 / math.sqrt(n_replica * n_expert * tok * top_count / EXPERTS)
    e = lax.axis_index("expert")
    z = lax.axis_index("replica")
    both = ("expert", "replica")

    def send(array, expert_to, moves):
        pairs = [
            (a * n_replica + i, expert_to(a) * n_replica + j)
            for a in range(n_expert)
            for i, j in moves
        ]
        return lax.ppermute(array, both, pairs)

    stay = [(i, i) for i in range(4)]
    near = [(0, 1), (1, 0), (2, 3), (3, 2)]
    middle = [(1, 2), (2, 1)]
    outward = [(1, 0), (2, 3)]
    same = lambda a: a
    inner = (z == 1) | (z == 2)

    own = grad_rows
    pair = send(own, same, near)
    mid_a = send(own, same, middle)
    mid_b = send(pair, same, middle)
    end_a = send(mid_a, same, outward)
    end_b = send(mid_b, same, outward)
    far_a = jnp.where(inner, mid_a, end_a)
    far_b = jnp.where(inner, mid_b, end_b)

    def around(rows):
        across = send(rows, lambda a: a ^ 2, stay)
        return [rows, send(rows, lambda a: a ^ 1, stay), across, send(across, lambda a: a ^ 1, stay)]

    ids = expert_ids.T
    named = ids[None, :, :] == jnp.arange(EXPERTS, dtype=jnp.int32)[:, None, None]
    mask = jnp.any(named, axis=1)
    coef = jnp.sum(jnp.where(named, (route_probs.T * grad_scale[None, :])[None], 0.0), axis=1)
    before = jnp.arange(tok)[:, None] < jnp.arange(tok)[None, :]
    place = jnp.dot(
        mask.astype(jnp.bfloat16), before.astype(jnp.bfloat16), preferred_element_type=jnp.float32
    )
    place = jnp.where(mask, place, -1.0)
    meta = jnp.stack([place, coef * scale_norm]).reshape(2, n_expert, per_device, tok)
    meta = lax.all_gather(meta, both, axis=0, tiled=False)
    meta = lax.dynamic_index_in_dim(meta, e, 2, keepdims=False)
    meta = meta.reshape(n_expert * n_replica, 2 * per_device, tok)

    def units_of(replica):
        return lax.dynamic_slice_in_dim(hidden, replica * units, units, 3)

    h_own = units_of(z)
    h_pair = send(units_of(z ^ 1), same, near)
    h_two = send(units_of(z ^ 2), same, [(i, i ^ 2) for i in range(4)])
    h_flip = send(units_of(z ^ 3), same, [(i, i ^ 3) for i in range(4)])

    def place_of(replica):
        return jnp.stack([e, replica]).astype(jnp.int32)

    s_own = spread(place_of(z), h_own, meta)
    s_pair = spread(place_of(z ^ 1), h_pair, meta)
    s_two = spread(place_of(z ^ 2), h_two, meta)
    s_flip = spread(place_of(z ^ 3), h_flip, meta)

    near_rows = around(own) + around(pair)
    rows_a, rows_b = around(far_a), around(far_b)
    ends = jnp.where(inner, 0, 1).astype(jnp.int32)[None]
    acc = product(ends, [s_own, s_pair], near_rows)
    acc = product(ends, [s_two], rows_a, rows_b, acc)
    return product(1 - ends, [s_flip], rows_a, rows_b, acc, last=True, experts=per_device)


def solution(mesh):
    placed = (
        P(("groups", "expert", "replica"), None),
        P(("groups", "expert", "replica")),
        P(("groups", "expert", "replica"), None),
        P(("groups", "expert", "replica"), None),
        P(("groups", "replica"), "expert", None, None, None),
    )
    small = mesh.shape["expert"] == 4 and mesh.shape["replica"] == 4
    return jax.shard_map(
        gathered_shards if small else summed_shards,
        mesh=mesh,
        in_specs=placed,
        out_specs=P(("groups", "replica"), "expert", None),
        check_vma=False,
    )
```

```python
import functools
import math

import jax
import jax.numpy as jnp
from jax import lax
from jax.experimental import pallas as pl
from jax.experimental.pallas import tpu as pltpu
from jax.sharding import PartitionSpec as P

EXPERTS = 16
ACC = jnp.bfloat16


def slot_positions(expert_ids):
    flat_ids = expert_ids.reshape(-1)
    onehot = (flat_ids[:, None] == jnp.arange(EXPERTS, dtype=jnp.int32)[None, :]).astype(jnp.int32)
    running = jnp.cumsum(onehot, axis=0)
    return (flat_ids, jnp.sum(onehot * running, axis=1) - 1)


def summed_shards(grad_rows, grad_scale, route_probs, expert_ids, saved_hidden):
    tok_rows, row_width = grad_rows.shape
    top_count = expert_ids.shape[1]
    n_expert = lax.axis_size("expert")
    n_replica = lax.axis_size("replica")
    per_device = EXPERTS // n_expert
    hidden = saved_hidden[0]
    capacity = hidden.shape[2]
    hidden_units = hidden.shape[3]
    scale_norm = 1.0 / math.sqrt(n_replica * n_expert * tok_rows * top_count / EXPERTS)
    flat_ids, position = slot_positions(expert_ids)
    pair_coef = grad_scale[:, None] * route_probs
    gathered_ids, gathered_pos = (
        lax.all_gather(expert_ids, "expert", axis=0, tiled=True),
        lax.all_gather(position.reshape(tok_rows, top_count), "expert", axis=0, tiled=True),
    )
    gathered_coef = lax.all_gather(pair_coef, "expert", axis=0, tiled=True)
    first_expert = lax.axis_index("expert") * per_device
    local_ids = first_expert + jnp.arange(per_device, dtype=jnp.int32)
    hidden_flat = hidden.reshape(per_device, n_expert * capacity, hidden_units)
    token_piece = lax.all_gather(grad_rows, "expert", axis=0, tiled=True)
    row_count = token_piece.shape[0]
    source = jnp.arange(row_count, dtype=jnp.int32) // tok_rows
    matches = gathered_ids[None, :, :] == local_ids[:, None, None]
    row_coef = jnp.sum(jnp.where(matches, gathered_coef[None], 0.0), axis=2)
    row_index = jnp.sum(
        jnp.where(matches, source[None, :, None] * capacity + gathered_pos[None], 0), axis=2
    )
    chosen = jax.vmap(lambda hidden_table, row_pick: jnp.take(hidden_table, row_pick, axis=0))(
        hidden_flat, row_index
    )
    scaled = (row_coef[:, :, None] * token_piece[None]).astype(jnp.bfloat16)
    summed = jnp.einsum("lif,lid->fld", chosen, scaled, preferred_element_type=jnp.float32)
    return lax.psum_scatter(
        (summed * scale_norm).astype(jnp.bfloat16), "replica", scatter_dimension=0, tiled=True
    )


def label_kernel(scale_norm, rows_ref, scale_ref, probs_ref, ids_ref, out_ref):
    tok, width = rows_ref.shape
    out_ref[:, :width] = rows_ref[...]
    coef = probs_ref[...] * scale_ref[...] * scale_norm
    ids = ids_ref[...]
    masks, coefs = [], []
    for j in range(EXPERTS):
        named = ids == j
        masks.append(jnp.sum(jnp.where(named, 1.0, 0.0), axis=0, keepdims=True))
        coefs.append(jnp.sum(jnp.where(named, coef, 0.0), axis=0, keepdims=True))
    mask = jnp.concatenate(masks, axis=0)
    coef = jnp.concatenate(coefs, axis=0)
    row = lax.broadcasted_iota(jnp.int32, (tok, tok), 0)
    col = lax.broadcasted_iota(jnp.int32, (tok, tok), 1)
    before = jnp.where(row < col, 1.0, 0.0).astype(jnp.bfloat16)
    place = jnp.dot(mask.astype(jnp.bfloat16), before, preferred_element_type=jnp.float32)
    place = jnp.where(mask > 0.0, place, -1.0)
    high = coef.astype(jnp.bfloat16).astype(jnp.float32)
    mid = (coef - high).astype(jnp.bfloat16).astype(jnp.float32)
    low = coef - high - mid
    rest = jnp.zeros((tok - 4 * EXPERTS, tok), jnp.float32)
    labels = jnp.concatenate([place, high, mid, low, rest], axis=0)
    out_ref[:, width:] = labels.T.astype(out_ref.dtype)


def labelled(grad_rows, grad_scale, route_probs, expert_ids, scale_norm):
    tok, width = grad_rows.shape
    return pl.pallas_call(
        functools.partial(label_kernel, scale_norm),
        out_shape=jax.ShapeDtypeStruct((tok, width + tok), grad_rows.dtype),
        compiler_params=pltpu.CompilerParams(vmem_limit_bytes=60 << 20),
    )(grad_rows, grad_scale[None, :], route_probs.T, expert_ids.T)


def spread_rows(me, hidden_ref, label_refs, out_ref, table_ref, rows_ref):
    experts, sources, capacity, units = hidden_ref.shape
    tok = label_refs[0].shape[0]
    slot = lax.broadcasted_iota(jnp.int32, (capacity, tok), 0).astype(jnp.float32)
    for q in range(sources):
        src = me ^ q
        table_ref[...] = label_refs[q][...].astype(jnp.float32).T
        for j in range(experts):
            line = lambda part: table_ref[pl.ds(part * EXPERTS + me * experts + j, 1), :]
            pos = line(0)
            coef = line(1) + line(2) + line(3)
            pick = jnp.where(slot == pos, 1.0, 0.0).astype(jnp.bfloat16)
            rows = lax.dot_general(
                hidden_ref[j, src],
                pick,
                (((0,), (0,)), ((), ())),
                preferred_element_type=jnp.float32,
            )
            rows_ref[pl.ds(j, units, stride=experts), :] = rows * coef
        out_ref[:, q * tok : (q + 1) * tok] = rows_ref[...].astype(out_ref.dtype)


def spread_call(body, where, hiddens, unit_blocks, labels, n_out):
    experts, sources, capacity = hiddens[0].shape[:3]
    tok = labels[0].shape[0]
    units = hiddens[0].shape[3] // unit_blocks
    last = labels[0].shape[1] // tok - 1
    out = jax.ShapeDtypeStruct((units * experts, sources * tok), jnp.bfloat16)
    out_spec = pl.BlockSpec(out.shape, lambda i, w: (0, 0))
    return pl.pallas_call(
        body,
        grid_spec=pltpu.PrefetchScalarGridSpec(
            num_scalar_prefetch=1,
            grid=(1,),
            in_specs=[
                pl.BlockSpec(
                    (experts, sources, capacity, units),
                    (lambda i, w: (0, 0, 0, w[1])) if unit_blocks > 1 else (lambda i, w: (0, 0, 0, 0)),
                )
                for _ in hiddens
            ]
            + [pl.BlockSpec((tok, tok), lambda i, w: (0, last)) for _ in labels],
            out_specs=[out_spec] * n_out,
            scratch_shapes=[
                pltpu.VMEM((tok, tok), jnp.float32),
                pltpu.VMEM((units * experts, tok), jnp.float32),
            ],
        ),
        out_shape=[out] * n_out,
        compiler_params=pltpu.CompilerParams(vmem_limit_bytes=16 << 20),
        cost_estimate=pl.CostEstimate(
            flops=4 * n_out * sources * tok * units * experts * capacity,
            bytes_accessed=n_out * (hiddens[0].size * 2 + out.size * 2),
            transcendentals=0,
        ),
    )(where, *hiddens, *labels)


def spread(where, hidden, unit_blocks, labels):
    def body(where_ref, hidden_ref, *refs):
        *label_refs, out_ref, table_ref, rows_ref = refs
        spread_rows(where_ref[0], hidden_ref, label_refs, out_ref, table_ref, rows_ref)

    return spread_call(body, where, [hidden], unit_blocks, labels, 1)[0]


def spread_far(where, hidden_ends, hidden_inner, labels_a, labels_b):
    def body(where_ref, ends_a, ends_b, inner_a, inner_b, *refs):
        *label_refs, out_a, out_b, table_ref, rows_ref = refs
        n = len(label_refs) // 2

        def both(hidden_a, hidden_b):
            spread_rows(where_ref[0], hidden_a, label_refs[:n], out_a, table_ref, rows_ref)
            spread_rows(where_ref[0], hidden_b, label_refs[n:], out_b, table_ref, rows_ref)

        @pl.when(where_ref[2] == 1)
        def _():
            both(ends_a, ends_b)

        @pl.when(where_ref[2] == 0)
        def _():
            both(inner_a, inner_b)

    return spread_call(
        body, where, [*hidden_ends, *hidden_inner], 1, [*labels_a, *labels_b], 2
    )


def product(spreads, rows, width, acc=None, last=False, experts=4, tile=512):
    n_tok = rows[0].shape[0]
    m = spreads[0].shape[0]
    k = sum(s.shape[1] for s in spreads)

    def body(*refs):
        refs = list(refs)
        lhs = [refs.pop(0) for _ in spreads]
        held = [refs.pop(0) for _ in rows]
        before = refs.pop(0) if acc is not None else None
        out = refs.pop(0)
        right = jnp.concatenate([r[...] for r in held], axis=0)
        left = jnp.concatenate([r[...] for r in lhs], axis=1) if len(lhs) > 1 else lhs[0][...]
        total = jnp.dot(left, right, preferred_element_type=jnp.float32)
        if before is not None:
            total = total + before[...].astype(jnp.float32)
        if last:
            out[...] = total.reshape(m // experts, experts, tile).astype(out.dtype)
        else:
            out[...] = total.astype(out.dtype)

    in_specs = [
        pl.BlockSpec(s.shape, lambda i: (0, 0), pipeline_mode=pl.Buffered(1)) for s in spreads
    ]
    in_specs += [pl.BlockSpec((n_tok, tile), lambda i: (0, i)) for _ in rows]
    args = [*spreads, *rows]
    if acc is not None:
        in_specs.append(pl.BlockSpec((m, tile), lambda i: (0, i)))
        args.append(acc)
    if last:
        out_shape = jax.ShapeDtypeStruct((m // experts, experts, width), jnp.bfloat16)
        out_spec = pl.BlockSpec((m // experts, experts, tile), lambda i: (0, 0, i))
    else:
        out_shape = jax.ShapeDtypeStruct((m, width), ACC)
        out_spec = pl.BlockSpec((m, tile), lambda i: (0, i))
    return pl.pallas_call(
        body,
        grid=(width // tile,),
        in_specs=in_specs,
        out_specs=out_spec,
        out_shape=out_shape,
        compiler_params=pltpu.CompilerParams(vmem_limit_bytes=20 << 20),
        cost_estimate=pl.CostEstimate(
            flops=2 * m * k * width,
            bytes_accessed=m * width * 4 + k * width * 2,
            transcendentals=0,
        ),
    )(*args)


def gathered_shards(grad_rows, grad_scale, route_probs, expert_ids, saved_hidden):
    tok, width = grad_rows.shape
    top_count = expert_ids.shape[1]
    n_expert = lax.axis_size("expert")
    n_replica = lax.axis_size("replica")
    per_device = EXPERTS // n_expert
    hidden = saved_hidden[0]
    units = hidden.shape[3] // n_replica
    scale_norm = 1.0 / math.sqrt(n_replica * n_expert * tok * top_count / EXPERTS)
    e = lax.axis_index("expert")
    z = lax.axis_index("replica")
    both = ("expert", "replica")

    def send(name, array, expert_to, moves):
        pairs = [
            (a * n_replica + i, expert_to(a) * n_replica + j)
            for a in range(n_expert)
            for i, j in moves
        ]
        with jax.named_scope(name):
            return lax.ppermute(array, both, pairs)

    stay = [(i, i) for i in range(4)]
    near = [(0, 1), (1, 0), (2, 3), (3, 2)]
    middle = [(1, 2), (2, 1)]
    outward = [(1, 0), (2, 3)]
    outer = [(0, 3), (3, 0)]
    cross_in = [(2, 0), (1, 3)]
    cross_out = [(0, 2), (3, 1)]
    same = lambda a: a
    core = lambda a: a ^ 1
    side = lambda a: a ^ 2
    inner = (z == 1) | (z == 2)

    def units_of(replica):
        return lax.dynamic_slice_in_dim(hidden, replica * units, units, 3)

    own = labelled(grad_rows, grad_scale, route_probs, expert_ids, scale_norm)

    tie = lax.optimization_barrier
    h_near, h_cross, h_flip = (units_of(z ^ i) for i in range(1, 4))

    where = jnp.stack([e, z, jnp.where(inner, 0, 1)]).astype(jnp.int32)

    c_own = send("c_own", own, core, stay)
    mid_a = send("mid_a", own, same, middle)
    x_own = send("x_own", own, side, stay)
    pair = send("pair", own, same, near)
    c_own, h_near, own, where, mid_a, h_flip, x_own, h_cross, pair = tie(
        (c_own, h_near, own, where, mid_a, h_flip, x_own, h_cross, pair)
    )

    end_a = send("end_a", mid_a, same, outward)
    mid_b = send("mid_b", pair, same, middle)
    x_pair = send("x_pair", pair, side, stay)
    g_near = send("g_near", h_near, same, near)
    g_inner = send("g_inner", h_flip, same, middle)
    far_a = jnp.where(inner, mid_a, end_a)
    x_pair, g_near, c_own, h_cross, x_own, pair, far_a, h_flip, g_inner, own, mid_b = tie(
        (x_pair, g_near, c_own, h_cross, x_own, pair, far_a, h_flip, g_inner, own, mid_b)
    )

    end_b = send("end_b", mid_b, same, outward)
    g_out = send("g_out", h_cross, same, cross_out)
    x_far_a = send("x_far_a", far_a, side, stay)
    c_xown = send("c_xown", x_own, core, stay)
    c_pair = send("c_pair", pair, core, stay)
    far_b = jnp.where(inner, mid_b, end_b)
    x_far_a, g_out, far_b, h_flip, far_a, pair, x_pair, c_xown, x_own, own, c_own, c_pair, h_cross = tie(
        (x_far_a, g_out, far_b, h_flip, far_a, pair, x_pair, c_xown, x_own, own, c_own, c_pair, h_cross)
    )

    g_outer = send("g_outer", h_flip, same, outer)
    g_in = send("g_in", h_cross, same, cross_in)
    x_far_b = send("x_far_b", far_b, side, stay)
    c_xpair = send("c_xpair", x_pair, core, stay)
    c_far_a = send("c_far_a", far_a, core, stay)
    rows_own = [own, c_own, x_own, c_xown]
    rows_near = [pair, c_pair, x_pair, c_xpair]
    s_own = spread(where, hidden, n_replica, rows_own)
    s_near = spread(where, g_near, 1, rows_near)
    acc = product([s_own, s_near], rows_own + rows_near, width)
    c_far_a, g_outer, x_far_b, acc, x_far_a, far_b, g_in = tie(
        (c_far_a, g_outer, x_far_b, acc, x_far_a, far_b, g_in)
    )

    c_xfar_a = send("c_xfar_a", x_far_a, core, stay)
    c_far_b = send("c_far_b", far_b, core, stay)
    c_xfar_b = send("c_xfar_b", x_far_b, core, stay)
    rows_a = [far_a, c_far_a, x_far_a, c_xfar_a]
    rows_b = [far_b, c_far_b, x_far_b, c_xfar_b]
    s_a, s_b = spread_far(where, (g_in, g_outer), (g_inner, g_out), rows_a, rows_b)
    return product([s_a, s_b], rows_a + rows_b, width, acc, last=True, experts=per_device)


def solution(mesh):
    placed = (
        P(("groups", "expert", "replica"), None),
        P(("groups", "expert", "replica")),
        P(("groups", "expert", "replica"), None),
        P(("groups", "expert", "replica"), None),
        P(("groups", "replica"), "expert", None, None, None),
    )
    small = mesh.shape["expert"] == 4 and mesh.shape["replica"] == 4
    return jax.shard_map(
        gathered_shards if small else summed_shards,
        mesh=mesh,
        in_specs=placed,
        out_specs=P(("groups", "replica"), "expert", None),
        check_vma=False,
    )
```

```python
import functools
import math

import jax
import jax.numpy as jnp
from jax import lax
from jax.experimental import pallas as pl
from jax.experimental.pallas import tpu as pltpu
from jax.sharding import PartitionSpec as P

EXPERTS = 16
ACC = jnp.bfloat16


def slot_positions(expert_ids):
    flat_ids = expert_ids.reshape(-1)
    onehot = (flat_ids[:, None] == jnp.arange(EXPERTS, dtype=jnp.int32)[None, :]).astype(jnp.int32)
    running = jnp.cumsum(onehot, axis=0)
    return (flat_ids, jnp.sum(onehot * running, axis=1) - 1)


def summed_shards(grad_rows, grad_scale, route_probs, expert_ids, saved_hidden):
    tok_rows, row_width = grad_rows.shape
    top_count = expert_ids.shape[1]
    n_expert = lax.axis_size("expert")
    n_replica = lax.axis_size("replica")
    per_device = EXPERTS // n_expert
    hidden = saved_hidden[0]
    capacity = hidden.shape[2]
    hidden_units = hidden.shape[3]
    scale_norm = 1.0 / math.sqrt(n_replica * n_expert * tok_rows * top_count / EXPERTS)
    flat_ids, position = slot_positions(expert_ids)
    pair_coef = grad_scale[:, None] * route_probs
    gathered_ids, gathered_pos = (
        lax.all_gather(expert_ids, "expert", axis=0, tiled=True),
        lax.all_gather(position.reshape(tok_rows, top_count), "expert", axis=0, tiled=True),
    )
    gathered_coef = lax.all_gather(pair_coef, "expert", axis=0, tiled=True)
    first_expert = lax.axis_index("expert") * per_device
    local_ids = first_expert + jnp.arange(per_device, dtype=jnp.int32)
    hidden_flat = hidden.reshape(per_device, n_expert * capacity, hidden_units)
    token_piece = lax.all_gather(grad_rows, "expert", axis=0, tiled=True)
    row_count = token_piece.shape[0]
    source = jnp.arange(row_count, dtype=jnp.int32) // tok_rows
    matches = gathered_ids[None, :, :] == local_ids[:, None, None]
    row_coef = jnp.sum(jnp.where(matches, gathered_coef[None], 0.0), axis=2)
    row_index = jnp.sum(
        jnp.where(matches, source[None, :, None] * capacity + gathered_pos[None], 0), axis=2
    )
    chosen = jax.vmap(lambda hidden_table, row_pick: jnp.take(hidden_table, row_pick, axis=0))(
        hidden_flat, row_index
    )
    scaled = (row_coef[:, :, None] * token_piece[None]).astype(jnp.bfloat16)
    summed = jnp.einsum("lif,lid->fld", chosen, scaled, preferred_element_type=jnp.float32)
    return lax.psum_scatter(
        (summed * scale_norm).astype(jnp.bfloat16), "replica", scatter_dimension=0, tiled=True
    )


def label_kernel(scale_norm, rows_ref, scale_ref, probs_ref, ids_ref, out_ref):
    tok, width = rows_ref.shape
    out_ref[:, :width] = rows_ref[...]
    coef = probs_ref[...] * scale_ref[...] * scale_norm
    ids = ids_ref[...]
    masks, coefs = [], []
    for j in range(EXPERTS):
        named = ids == j
        masks.append(jnp.sum(jnp.where(named, 1.0, 0.0), axis=0, keepdims=True))
        coefs.append(jnp.sum(jnp.where(named, coef, 0.0), axis=0, keepdims=True))
    mask = jnp.concatenate(masks, axis=0)
    coef = jnp.concatenate(coefs, axis=0)
    row = lax.broadcasted_iota(jnp.int32, (tok, tok), 0)
    col = lax.broadcasted_iota(jnp.int32, (tok, tok), 1)
    before = jnp.where(row < col, 1.0, 0.0).astype(jnp.bfloat16)
    place = jnp.dot(mask.astype(jnp.bfloat16), before, preferred_element_type=jnp.float32)
    place = jnp.where(mask > 0.0, place, -1.0)
    high = coef.astype(jnp.bfloat16).astype(jnp.float32)
    mid = (coef - high).astype(jnp.bfloat16).astype(jnp.float32)
    low = coef - high - mid
    rest = jnp.zeros((tok - 4 * EXPERTS, tok), jnp.float32)
    labels = jnp.concatenate([place, high, mid, low, rest], axis=0)
    out_ref[:, width:] = labels.T.astype(out_ref.dtype)


def labelled(grad_rows, grad_scale, route_probs, expert_ids, scale_norm):
    tok, width = grad_rows.shape
    return pl.pallas_call(
        functools.partial(label_kernel, scale_norm),
        out_shape=jax.ShapeDtypeStruct((tok, width + tok), grad_rows.dtype),
        compiler_params=pltpu.CompilerParams(vmem_limit_bytes=60 << 20),
    )(grad_rows, grad_scale[None, :], route_probs.T, expert_ids.T)


def spread_rows(me, hidden_ref, label_refs, out_ref, table_ref, rows_ref):
    experts, sources, capacity, units = hidden_ref.shape
    tok = label_refs[0].shape[0]
    slot = lax.broadcasted_iota(jnp.int32, (capacity, tok), 0).astype(jnp.float32)
    for q in range(sources):
        src = me ^ q
        table_ref[...] = label_refs[q][...].astype(jnp.float32).T
        for j in range(experts):
            line = lambda part: table_ref[pl.ds(part * EXPERTS + me * experts + j, 1), :]
            pos = line(0)
            coef = line(1) + line(2) + line(3)
            pick = jnp.where(slot == pos, 1.0, 0.0).astype(jnp.bfloat16)
            rows = lax.dot_general(
                hidden_ref[j, src],
                pick,
                (((0,), (0,)), ((), ())),
                preferred_element_type=jnp.float32,
            )
            rows_ref[pl.ds(j, units, stride=experts), :] = rows * coef
        out_ref[:, q * tok : (q + 1) * tok] = rows_ref[...].astype(out_ref.dtype)


def last_block(label, tok):
    last = label.shape[1] // tok - 1
    return pl.BlockSpec((tok, tok), lambda i, w: (0, last))


def spread_call(body, where, hiddens, unit_blocks, labels, n_out):
    experts, sources, capacity = hiddens[0].shape[:3]
    tok = labels[0].shape[0]
    units = hiddens[0].shape[3] // unit_blocks
    out = jax.ShapeDtypeStruct((units * experts, sources * tok), jnp.bfloat16)
    out_spec = pl.BlockSpec(out.shape, lambda i, w: (0, 0))
    return pl.pallas_call(
        body,
        grid_spec=pltpu.PrefetchScalarGridSpec(
            num_scalar_prefetch=1,
            grid=(1,),
            in_specs=[
                pl.BlockSpec(
                    (experts, sources, capacity, units),
                    (lambda i, w: (0, 0, 0, w[1])) if unit_blocks > 1 else (lambda i, w: (0, 0, 0, 0)),
                )
                for _ in hiddens
            ]
            + [last_block(label, tok) for label in labels],
            out_specs=[out_spec] * n_out,
            scratch_shapes=[
                pltpu.VMEM((tok, tok), jnp.float32),
                pltpu.VMEM((units * experts, tok), jnp.float32),
            ],
        ),
        out_shape=[out] * n_out,
        compiler_params=pltpu.CompilerParams(vmem_limit_bytes=16 << 20),
        cost_estimate=pl.CostEstimate(
            flops=4 * n_out * sources * tok * units * experts * capacity,
            bytes_accessed=n_out * (hiddens[0].size * 2 + out.size * 2),
            transcendentals=0,
        ),
    )(where, *hiddens, *labels)


def spread(where, hidden, unit_blocks, labels):
    def body(where_ref, hidden_ref, *refs):
        *label_refs, out_ref, table_ref, rows_ref = refs
        spread_rows(where_ref[0], hidden_ref, label_refs, out_ref, table_ref, rows_ref)

    return spread_call(body, where, [hidden], unit_blocks, labels, 1)[0]


def spread_far(where, hidden_ends, hidden_inner, labels):
    def body(where_ref, ends_ref, inner_ref, *refs):
        *label_refs, out_ref, table_ref, rows_ref = refs

        @pl.when(where_ref[2] == 1)
        def _():
            spread_rows(where_ref[0], ends_ref, label_refs, out_ref, table_ref, rows_ref)

        @pl.when(where_ref[2] == 0)
        def _():
            spread_rows(where_ref[0], inner_ref, label_refs, out_ref, table_ref, rows_ref)

    return spread_call(body, where, [hidden_ends, hidden_inner], 1, labels, 1)[0]


def product(spreads, rows, width, acc=None, last=False, experts=4, tile=512):
    n_tok = rows[0].shape[0]
    m = spreads[0].shape[0]
    k = sum(s.shape[1] for s in spreads)

    def body(*refs):
        refs = list(refs)
        lhs = [refs.pop(0) for _ in spreads]
        held = [refs.pop(0) for _ in rows]
        before = refs.pop(0) if acc is not None else None
        out = refs.pop(0)
        right = jnp.concatenate([r[...] for r in held], axis=0)
        left = jnp.concatenate([r[...] for r in lhs], axis=1) if len(lhs) > 1 else lhs[0][...]
        total = jnp.dot(left, right, preferred_element_type=jnp.float32)
        if before is not None:
            total = total + before[...].astype(jnp.float32)
        if last:
            out[...] = total.reshape(m // experts, experts, tile).astype(out.dtype)
        else:
            out[...] = total.astype(out.dtype)

    in_specs = [
        pl.BlockSpec(s.shape, lambda i: (0, 0), pipeline_mode=pl.Buffered(1)) for s in spreads
    ]
    in_specs += [pl.BlockSpec((n_tok, tile), lambda i: (0, i)) for _ in rows]
    args = [*spreads, *rows]
    if acc is not None:
        in_specs.append(pl.BlockSpec((m, tile), lambda i: (0, i)))
        args.append(acc)
    if last:
        out_shape = jax.ShapeDtypeStruct((m // experts, experts, width), jnp.bfloat16)
        out_spec = pl.BlockSpec((m // experts, experts, tile), lambda i: (0, 0, i))
    else:
        out_shape = jax.ShapeDtypeStruct((m, width), ACC)
        out_spec = pl.BlockSpec((m, tile), lambda i: (0, i))
    return pl.pallas_call(
        body,
        grid=(width // tile,),
        in_specs=in_specs,
        out_specs=out_spec,
        out_shape=out_shape,
        compiler_params=pltpu.CompilerParams(vmem_limit_bytes=20 << 20),
        cost_estimate=pl.CostEstimate(
            flops=2 * m * k * width,
            bytes_accessed=m * width * 4 + k * width * 2,
            transcendentals=0,
        ),
    )(*args)


def gathered_shards(grad_rows, grad_scale, route_probs, expert_ids, saved_hidden):
    tok, width = grad_rows.shape
    top_count = expert_ids.shape[1]
    n_expert = lax.axis_size("expert")
    n_replica = lax.axis_size("replica")
    per_device = EXPERTS // n_expert
    hidden = saved_hidden[0]
    units = hidden.shape[3] // n_replica
    scale_norm = 1.0 / math.sqrt(n_replica * n_expert * tok * top_count / EXPERTS)
    e = lax.axis_index("expert")
    z = lax.axis_index("replica")
    both = ("expert", "replica")

    def send(name, array, expert_to, moves):
        pairs = [
            (a * n_replica + i, expert_to(a) * n_replica + j)
            for a in range(n_expert)
            for i, j in moves
        ]
        with jax.named_scope(name):
            return lax.ppermute(array, both, pairs)

    stay = [(i, i) for i in range(4)]
    near = [(0, 1), (1, 0), (2, 3), (3, 2)]
    middle = [(1, 2), (2, 1)]
    outward = [(1, 0), (2, 3)]
    outer = [(0, 3), (3, 0)]
    cross_in = [(2, 0), (1, 3)]
    cross_out = [(0, 2), (3, 1)]
    same = lambda a: a
    core = lambda a: a ^ 1
    side = lambda a: a ^ 2
    inner = (z == 1) | (z == 2)

    def units_of(replica):
        return lax.dynamic_slice_in_dim(hidden, replica * units, units, 3)

    own = labelled(grad_rows, grad_scale, route_probs, expert_ids, scale_norm)

    tie = lax.optimization_barrier
    h_near, h_cross, h_flip = (units_of(z ^ i) for i in range(1, 4))
    where = jnp.stack([e, z, jnp.where(inner, 0, 1)]).astype(jnp.int32)

    c_own = send("c_own", own, core, stay)
    mid_a = send("mid_a", own, same, middle)
    x_own = send("x_own", own, side, stay)
    pair = send("pair", own, same, near)
    c_own, own, h_flip, h_near, mid_a, h_cross, pair, x_own, where = tie(
        (c_own, own, h_flip, h_near, mid_a, h_cross, pair, x_own, where)
    )

    end_a = send("end_a", mid_a, same, outward)
    mid_b = send("mid_b", pair, same, middle)
    x_pair = send("x_pair", pair, side, stay)
    g_near = send("g_near", h_near, same, near)
    g_inner = send("g_inner", h_flip, same, middle)
    c_xown = send("c_xown", x_own, core, stay)
    far_a = jnp.where(inner, mid_a, end_a)
    c_own, x_pair, pair, own, g_inner, mid_b, far_a, h_flip, c_xown, h_cross, x_own, g_near = tie(
        (c_own, x_pair, pair, own, g_inner, mid_b, far_a, h_flip, c_xown, h_cross, x_own, g_near)
    )

    end_b = send("end_b", mid_b, same, outward)
    g_out = send("g_out", h_cross, same, cross_out)
    x_far_a = send("x_far_a", far_a, side, stay)
    c_xpair = send("c_xpair", x_pair, core, stay)
    c_pair = send("c_pair", pair, core, stay)
    l_xfar_a = x_far_a[:, width:]
    s_own = spread(where, hidden, n_replica, [own, c_own, x_own, c_xown])
    far_b = jnp.where(inner, mid_b, end_b)
    c_xpair, c_pair, h_cross, h_flip, pair, x_far_a, s_own, c_xown, far_b, c_own, far_a, x_own, l_xfar_a, g_out, own, x_pair = tie(
        (c_xpair, c_pair, h_cross, h_flip, pair, x_far_a, s_own, c_xown, far_b, c_own, far_a, x_own, l_xfar_a, g_out, own, x_pair)
    )

    g_outer = send("g_outer", h_flip, same, outer)
    g_in = send("g_in", h_cross, same, cross_in)
    x_far_b = send("x_far_b", far_b, side, stay)
    c_far_a = send("c_far_a", far_a, core, stay)
    c_xfar_a = send("c_xfar_a", x_far_a, core, stay)
    rows_own = [own, c_own, x_own, c_xown]
    rows_near = [pair, c_pair, x_pair, c_xpair]
    s_near = spread(where, g_near, 1, rows_near)
    acc = product([s_own, s_near], rows_own + rows_near, width)
    c_far_b = send("c_far_b", far_b, core, stay)
    s_a = spread_far(where, g_in, g_inner, [far_a, c_far_a, l_xfar_a, c_xfar_a])
    far_b, s_a, g_outer, x_far_b, acc, c_xfar_a, c_far_a, c_far_b = tie(
        (far_b, s_a, g_outer, x_far_b, acc, c_xfar_a, c_far_a, c_far_b)
    )

    c_xfar_b = send("c_xfar_b", x_far_b, core, stay)
    rows_a = [far_a, c_far_a, x_far_a, c_xfar_a]
    rows_b = [far_b, c_far_b, x_far_b, c_xfar_b]
    s_b = spread_far(where, g_outer, g_out, rows_b)
    return product([s_a, s_b], rows_a + rows_b, width, acc, last=True, experts=per_device)


def solution(mesh):
    placed = (
        P(("groups", "expert", "replica"), None),
        P(("groups", "expert", "replica")),
        P(("groups", "expert", "replica"), None),
        P(("groups", "expert", "replica"), None),
        P(("groups", "replica"), "expert", None, None, None),
    )
    small = mesh.shape["expert"] == 4 and mesh.shape["replica"] == 4
    return jax.shard_map(
        gathered_shards if small else summed_shards,
        mesh=mesh,
        in_specs=placed,
        out_specs=P(("groups", "replica"), "expert", None),
        check_vma=False,
    )
```

```python
import functools
import math

import jax
import jax.numpy as jnp
from jax import lax
from jax.experimental import pallas as pl
from jax.experimental.pallas import tpu as pltpu
from jax.sharding import PartitionSpec as P

EXPERTS = 16
ACC = jnp.bfloat16


def slot_positions(expert_ids):
    flat_ids = expert_ids.reshape(-1)
    onehot = (flat_ids[:, None] == jnp.arange(EXPERTS, dtype=jnp.int32)[None, :]).astype(jnp.int32)
    running = jnp.cumsum(onehot, axis=0)
    return (flat_ids, jnp.sum(onehot * running, axis=1) - 1)


def summed_shards(grad_rows, grad_scale, route_probs, expert_ids, saved_hidden):
    tok_rows, row_width = grad_rows.shape
    top_count = expert_ids.shape[1]
    n_expert = lax.axis_size("expert")
    n_replica = lax.axis_size("replica")
    per_device = EXPERTS // n_expert
    hidden = saved_hidden[0]
    capacity = hidden.shape[2]
    hidden_units = hidden.shape[3]
    scale_norm = 1.0 / math.sqrt(n_replica * n_expert * tok_rows * top_count / EXPERTS)
    flat_ids, position = slot_positions(expert_ids)
    pair_coef = grad_scale[:, None] * route_probs
    gathered_ids, gathered_pos = (
        lax.all_gather(expert_ids, "expert", axis=0, tiled=True),
        lax.all_gather(position.reshape(tok_rows, top_count), "expert", axis=0, tiled=True),
    )
    gathered_coef = lax.all_gather(pair_coef, "expert", axis=0, tiled=True)
    first_expert = lax.axis_index("expert") * per_device
    local_ids = first_expert + jnp.arange(per_device, dtype=jnp.int32)
    hidden_flat = hidden.reshape(per_device, n_expert * capacity, hidden_units)
    token_piece = lax.all_gather(grad_rows, "expert", axis=0, tiled=True)
    row_count = token_piece.shape[0]
    source = jnp.arange(row_count, dtype=jnp.int32) // tok_rows
    matches = gathered_ids[None, :, :] == local_ids[:, None, None]
    row_coef = jnp.sum(jnp.where(matches, gathered_coef[None], 0.0), axis=2)
    row_index = jnp.sum(
        jnp.where(matches, source[None, :, None] * capacity + gathered_pos[None], 0), axis=2
    )
    chosen = jax.vmap(lambda hidden_table, row_pick: jnp.take(hidden_table, row_pick, axis=0))(
        hidden_flat, row_index
    )
    scaled = (row_coef[:, :, None] * token_piece[None]).astype(jnp.bfloat16)
    summed = jnp.einsum("lif,lid->fld", chosen, scaled, preferred_element_type=jnp.float32)
    return lax.psum_scatter(
        (summed * scale_norm).astype(jnp.bfloat16), "replica", scatter_dimension=0, tiled=True
    )


def label_kernel(scale_norm, rows_ref, scale_ref, probs_ref, ids_ref, out_ref):
    tok, width = rows_ref.shape
    out_ref[:, :width] = rows_ref[...]
    coef = probs_ref[...] * scale_ref[...] * scale_norm
    ids = ids_ref[...]
    masks, coefs = [], []
    for j in range(EXPERTS):
        named = ids == j
        masks.append(jnp.sum(jnp.where(named, 1.0, 0.0), axis=0, keepdims=True))
        coefs.append(jnp.sum(jnp.where(named, coef, 0.0), axis=0, keepdims=True))
    mask = jnp.concatenate(masks, axis=0)
    coef = jnp.concatenate(coefs, axis=0)
    row = lax.broadcasted_iota(jnp.int32, (tok, tok), 0)
    col = lax.broadcasted_iota(jnp.int32, (tok, tok), 1)
    before = jnp.where(row < col, 1.0, 0.0).astype(jnp.bfloat16)
    place = jnp.dot(mask.astype(jnp.bfloat16), before, preferred_element_type=jnp.float32)
    place = jnp.where(mask > 0.0, place, -1.0)
    high = coef.astype(jnp.bfloat16).astype(jnp.float32)
    mid = (coef - high).astype(jnp.bfloat16).astype(jnp.float32)
    low = coef - high - mid
    rest = jnp.zeros((tok - 4 * EXPERTS, tok), jnp.float32)
    labels = jnp.concatenate([place, high, mid, low, rest], axis=0)
    out_ref[:, width:] = labels.T.astype(out_ref.dtype)


def labelled(grad_rows, grad_scale, route_probs, expert_ids, scale_norm):
    tok, width = grad_rows.shape
    return pl.pallas_call(
        functools.partial(label_kernel, scale_norm),
        out_shape=jax.ShapeDtypeStruct((tok, width + tok), grad_rows.dtype),
        compiler_params=pltpu.CompilerParams(vmem_limit_bytes=60 << 20),
    )(grad_rows, grad_scale[None, :], route_probs.T, expert_ids.T)


def spread_rows(me, hidden_ref, label_refs, out_ref, table_ref, rows_ref):
    experts, sources, capacity, units = hidden_ref.shape
    tok = label_refs[0].shape[0]
    slot = lax.broadcasted_iota(jnp.int32, (capacity, tok), 0).astype(jnp.float32)
    for q in range(sources):
        src = me ^ q
        table_ref[...] = label_refs[q][...].astype(jnp.float32).T
        for j in range(experts):
            line = lambda part: table_ref[pl.ds(part * EXPERTS + me * experts + j, 1), :]
            pos = line(0)
            coef = line(1) + line(2) + line(3)
            pick = jnp.where(slot == pos, 1.0, 0.0).astype(jnp.bfloat16)
            rows = lax.dot_general(
                hidden_ref[j, src],
                pick,
                (((0,), (0,)), ((), ())),
                preferred_element_type=jnp.float32,
            )
            rows_ref[pl.ds(j, units, stride=experts), :] = rows * coef
        out_ref[:, q * tok : (q + 1) * tok] = rows_ref[...].astype(out_ref.dtype)


def last_block(label, tok):
    last = label.shape[1] // tok - 1
    return pl.BlockSpec((tok, tok), lambda i, w: (0, last))


def spread_call(body, where, hiddens, unit_blocks, labels, n_out):
    experts, sources, capacity = hiddens[0].shape[:3]
    tok = labels[0].shape[0]
    units = hiddens[0].shape[3] // unit_blocks
    out = jax.ShapeDtypeStruct((units * experts, sources * tok), jnp.bfloat16)
    out_spec = pl.BlockSpec(out.shape, lambda i, w: (0, 0))
    return pl.pallas_call(
        body,
        grid_spec=pltpu.PrefetchScalarGridSpec(
            num_scalar_prefetch=1,
            grid=(1,),
            in_specs=[
                pl.BlockSpec(
                    (experts, sources, capacity, units),
                    (lambda i, w: (0, 0, 0, w[1])) if unit_blocks > 1 else (lambda i, w: (0, 0, 0, 0)),
                )
                for _ in hiddens
            ]
            + [last_block(label, tok) for label in labels],
            out_specs=[out_spec] * n_out,
            scratch_shapes=[
                pltpu.VMEM((tok, tok), jnp.float32),
                pltpu.VMEM((units * experts, tok), jnp.float32),
            ],
        ),
        out_shape=[out] * n_out,
        compiler_params=pltpu.CompilerParams(vmem_limit_bytes=16 << 20),
        cost_estimate=pl.CostEstimate(
            flops=4 * n_out * sources * tok * units * experts * capacity,
            bytes_accessed=n_out * (hiddens[0].size * 2 + out.size * 2),
            transcendentals=0,
        ),
    )(where, *hiddens, *labels)


def spread(where, hidden, unit_blocks, labels):
    def body(where_ref, hidden_ref, *refs):
        *label_refs, out_ref, table_ref, rows_ref = refs
        spread_rows(where_ref[0], hidden_ref, label_refs, out_ref, table_ref, rows_ref)

    return spread_call(body, where, [hidden], unit_blocks, labels, 1)[0]


def spread_far(where, hidden_ends, hidden_inner, labels):
    def body(where_ref, ends_ref, inner_ref, *refs):
        *label_refs, out_ref, table_ref, rows_ref = refs

        @pl.when(where_ref[2] == 1)
        def _():
            spread_rows(where_ref[0], ends_ref, label_refs, out_ref, table_ref, rows_ref)

        @pl.when(where_ref[2] == 0)
        def _():
            spread_rows(where_ref[0], inner_ref, label_refs, out_ref, table_ref, rows_ref)

    return spread_call(body, where, [hidden_ends, hidden_inner], 1, labels, 1)[0]


def product(spreads, rows, width, acc=None, last=False, experts=4, tile=512, cost=1):
    n_tok = rows[0].shape[0]
    m = spreads[0].shape[0]
    k = sum(s.shape[1] for s in spreads)

    def body(*refs):
        refs = list(refs)
        lhs = [refs.pop(0) for _ in spreads]
        held = [refs.pop(0) for _ in rows]
        before = refs.pop(0) if acc is not None else None
        out = refs.pop(0)
        right = jnp.concatenate([r[...] for r in held], axis=0)
        left = jnp.concatenate([r[...] for r in lhs], axis=1) if len(lhs) > 1 else lhs[0][...]
        total = jnp.dot(left, right, preferred_element_type=jnp.float32)
        if before is not None:
            total = total + before[...].astype(jnp.float32)
        if last:
            out[...] = total.reshape(m // experts, experts, tile).astype(out.dtype)
        else:
            out[...] = total.astype(out.dtype)

    in_specs = [
        pl.BlockSpec(s.shape, lambda i: (0, 0), pipeline_mode=pl.Buffered(1)) for s in spreads
    ]
    in_specs += [pl.BlockSpec((n_tok, tile), lambda i: (0, i)) for _ in rows]
    args = [*spreads, *rows]
    if acc is not None:
        in_specs.append(pl.BlockSpec((m, tile), lambda i: (0, i)))
        args.append(acc)
    if last:
        out_shape = jax.ShapeDtypeStruct((m // experts, experts, width), jnp.bfloat16)
        out_spec = pl.BlockSpec((m // experts, experts, tile), lambda i: (0, 0, i))
    else:
        out_shape = jax.ShapeDtypeStruct((m, width), ACC)
        out_spec = pl.BlockSpec((m, tile), lambda i: (0, i))
    return pl.pallas_call(
        body,
        grid=(width // tile,),
        in_specs=in_specs,
        out_specs=out_spec,
        out_shape=out_shape,
        compiler_params=pltpu.CompilerParams(vmem_limit_bytes=20 << 20),
        cost_estimate=pl.CostEstimate(
            flops=cost * 2 * m * k * width,
            bytes_accessed=cost * (m * width * 4 + k * width * 2),
            transcendentals=0,
        ),
    )(*args)


def gathered_shards(grad_rows, grad_scale, route_probs, expert_ids, saved_hidden):
    tok, width = grad_rows.shape
    top_count = expert_ids.shape[1]
    n_expert = lax.axis_size("expert")
    n_replica = lax.axis_size("replica")
    per_device = EXPERTS // n_expert
    hidden = saved_hidden[0]
    units = hidden.shape[3] // n_replica
    scale_norm = 1.0 / math.sqrt(n_replica * n_expert * tok * top_count / EXPERTS)
    e = lax.axis_index("expert")
    z = lax.axis_index("replica")
    both = ("expert", "replica")

    def send(name, array, expert_to, moves):
        pairs = [
            (a * n_replica + i, expert_to(a) * n_replica + j)
            for a in range(n_expert)
            for i, j in moves
        ]
        with jax.named_scope(name):
            return lax.ppermute(array, both, pairs)

    stay = [(i, i) for i in range(4)]
    near = [(0, 1), (1, 0), (2, 3), (3, 2)]
    middle = [(1, 2), (2, 1)]
    outward = [(1, 0), (2, 3)]
    outer = [(0, 3), (3, 0)]
    cross_in = [(2, 0), (1, 3)]
    cross_out = [(0, 2), (3, 1)]
    same = lambda a: a
    core = lambda a: a ^ 1
    side = lambda a: a ^ 2
    inner = (z == 1) | (z == 2)

    def units_of(replica):
        return lax.dynamic_slice_in_dim(hidden, replica * units, units, 3)

    own = labelled(grad_rows, grad_scale, route_probs, expert_ids, scale_norm)

    tie = lax.optimization_barrier
    h_near, h_cross, h_flip = (units_of(z ^ i) for i in range(1, 4))
    where = jnp.stack([e, z, jnp.where(inner, 0, 1)]).astype(jnp.int32)

    c_own = send("c_own", own, core, stay)
    mid_a = send("mid_a", own, same, middle)
    x_own = send("x_own", own, side, stay)
    pair = send("pair", own, same, near)
    own, c_own, mid_a, x_own, pair, where, h_near, h_cross, h_flip = tie(
        (own, c_own, mid_a, x_own, pair, where, h_near, h_cross, h_flip)
    )

    end_a = send("end_a", mid_a, same, outward)
    mid_b = send("mid_b", pair, same, middle)
    x_pair = send("x_pair", pair, side, stay)
    g_near = send("g_near", h_near, same, near)
    g_inner = send("g_inner", h_flip, same, middle)
    c_xown = send("c_xown", x_own, core, stay)
    far_a = jnp.where(inner, mid_a, end_a)
    x_pair, g_near, g_inner, c_xown, far_a, mid_b, own, c_own, x_own, pair, h_cross, h_flip = tie(
        (x_pair, g_near, g_inner, c_xown, far_a, mid_b, own, c_own, x_own, pair, h_cross, h_flip)
    )

    end_b = send("end_b", mid_b, same, outward)
    g_out = send("g_out", h_cross, same, cross_out)
    x_far_a = send("x_far_a", far_a, side, stay)
    c_xpair = send("c_xpair", x_pair, core, stay)
    c_pair = send("c_pair", pair, core, stay)
    l_xfar_a = x_far_a[:, width:]
    s_own = spread(where, hidden, n_replica, [own, c_own, x_own, c_xown])
    acc = product([s_own], [own, c_own, x_own, c_xown], width)
    far_b = jnp.where(inner, mid_b, end_b)
    far_b, x_far_a, l_xfar_a, g_out, c_xpair, c_pair, acc, pair, x_pair, far_a, h_cross, h_flip = tie(
        (far_b, x_far_a, l_xfar_a, g_out, c_xpair, c_pair, acc, pair, x_pair, far_a, h_cross, h_flip)
    )

    x_far_b = send("x_far_b", far_b, side, stay)
    g_in = send("g_in", h_cross, same, cross_in)
    c_far_a = send("c_far_a", far_a, core, stay)
    c_xfar_a = send("c_xfar_a", x_far_a, core, stay)
    rows_near = [pair, c_pair, x_pair, c_xpair]
    s_near = spread(where, g_near, 1, rows_near)
    acc = product([s_near], rows_near, width, acc, cost=4)
    g_in, acc, h_flip, far_b = tie(
        (g_in, acc, h_flip, far_b)
    )

    g_outer = send("g_outer", h_flip, same, outer)
    c_far_b = send("c_far_b", far_b, core, stay)
    s_a = spread_far(where, g_in, g_inner, [far_a, c_far_a, l_xfar_a, c_xfar_a])
    acc = product([s_a], [far_a, c_far_a, x_far_a, c_xfar_a], width, acc)
    g_outer, x_far_b, c_far_b, acc, far_b = tie(
        (g_outer, x_far_b, c_far_b, acc, far_b)
    )

    c_xfar_b = send("c_xfar_b", x_far_b, core, stay)
    rows_b = [far_b, c_far_b, x_far_b, c_xfar_b]
    s_b = spread_far(where, g_outer, g_out, rows_b)
    return product([s_b], rows_b, width, acc, last=True, experts=per_device)


def solution(mesh):
    placed = (
        P(("groups", "expert", "replica"), None),
        P(("groups", "expert", "replica")),
        P(("groups", "expert", "replica"), None),
        P(("groups", "expert", "replica"), None),
        P(("groups", "replica"), "expert", None, None, None),
    )
    small = mesh.shape["expert"] == 4 and mesh.shape["replica"] == 4
    return jax.shard_map(
        gathered_shards if small else summed_shards,
        mesh=mesh,
        in_specs=placed,
        out_specs=P(("groups", "replica"), "expert", None),
        check_vma=False,
    )
```

```python
import functools
import math

import jax
import jax.numpy as jnp
from jax import lax
from jax.experimental import pallas as pl
from jax.experimental.pallas import tpu as pltpu
from jax.sharding import PartitionSpec as P

EXPERTS = 16
ACC = jnp.bfloat16


def slot_positions(expert_ids):
    flat_ids = expert_ids.reshape(-1)
    onehot = (flat_ids[:, None] == jnp.arange(EXPERTS, dtype=jnp.int32)[None, :]).astype(jnp.int32)
    running = jnp.cumsum(onehot, axis=0)
    return (flat_ids, jnp.sum(onehot * running, axis=1) - 1)


def summed_shards(grad_rows, grad_scale, route_probs, expert_ids, saved_hidden):
    tok_rows, row_width = grad_rows.shape
    top_count = expert_ids.shape[1]
    n_expert = lax.axis_size("expert")
    n_replica = lax.axis_size("replica")
    per_device = EXPERTS // n_expert
    hidden = saved_hidden[0]
    capacity = hidden.shape[2]
    hidden_units = hidden.shape[3]
    scale_norm = 1.0 / math.sqrt(n_replica * n_expert * tok_rows * top_count / EXPERTS)
    flat_ids, position = slot_positions(expert_ids)
    pair_coef = grad_scale[:, None] * route_probs
    gathered_ids, gathered_pos = (
        lax.all_gather(expert_ids, "expert", axis=0, tiled=True),
        lax.all_gather(position.reshape(tok_rows, top_count), "expert", axis=0, tiled=True),
    )
    gathered_coef = lax.all_gather(pair_coef, "expert", axis=0, tiled=True)
    first_expert = lax.axis_index("expert") * per_device
    local_ids = first_expert + jnp.arange(per_device, dtype=jnp.int32)
    hidden_flat = hidden.reshape(per_device, n_expert * capacity, hidden_units)
    token_piece = lax.all_gather(grad_rows, "expert", axis=0, tiled=True)
    row_count = token_piece.shape[0]
    source = jnp.arange(row_count, dtype=jnp.int32) // tok_rows
    matches = gathered_ids[None, :, :] == local_ids[:, None, None]
    row_coef = jnp.sum(jnp.where(matches, gathered_coef[None], 0.0), axis=2)
    row_index = jnp.sum(
        jnp.where(matches, source[None, :, None] * capacity + gathered_pos[None], 0), axis=2
    )
    chosen = jax.vmap(lambda hidden_table, row_pick: jnp.take(hidden_table, row_pick, axis=0))(
        hidden_flat, row_index
    )
    scaled = (row_coef[:, :, None] * token_piece[None]).astype(jnp.bfloat16)
    summed = jnp.einsum("lif,lid->fld", chosen, scaled, preferred_element_type=jnp.float32)
    return lax.psum_scatter(
        (summed * scale_norm).astype(jnp.bfloat16), "replica", scatter_dimension=0, tiled=True
    )


def label_kernel(scale_norm, rows_ref, scale_ref, probs_ref, ids_ref, out_ref):
    tok, width = rows_ref.shape
    out_ref[:, :width] = rows_ref[...]
    coef = probs_ref[...] * scale_ref[...] * scale_norm
    ids = ids_ref[...]
    masks, coefs = [], []
    for j in range(EXPERTS):
        named = ids == j
        masks.append(jnp.sum(jnp.where(named, 1.0, 0.0), axis=0, keepdims=True))
        coefs.append(jnp.sum(jnp.where(named, coef, 0.0), axis=0, keepdims=True))
    mask = jnp.concatenate(masks, axis=0)
    coef = jnp.concatenate(coefs, axis=0)
    row = lax.broadcasted_iota(jnp.int32, (tok, tok), 0)
    col = lax.broadcasted_iota(jnp.int32, (tok, tok), 1)
    before = jnp.where(row < col, 1.0, 0.0).astype(jnp.bfloat16)
    place = jnp.dot(mask.astype(jnp.bfloat16), before, preferred_element_type=jnp.float32)
    place = jnp.where(mask > 0.0, place, -1.0)
    high = coef.astype(jnp.bfloat16).astype(jnp.float32)
    mid = (coef - high).astype(jnp.bfloat16).astype(jnp.float32)
    low = coef - high - mid
    rest = jnp.zeros((tok - 4 * EXPERTS, tok), jnp.float32)
    labels = jnp.concatenate([place, high, mid, low, rest], axis=0)
    out_ref[:, width:] = labels.T.astype(out_ref.dtype)


def labelled(grad_rows, grad_scale, route_probs, expert_ids, scale_norm):
    tok, width = grad_rows.shape
    return pl.pallas_call(
        functools.partial(label_kernel, scale_norm),
        out_shape=jax.ShapeDtypeStruct((tok, width + tok), grad_rows.dtype),
        compiler_params=pltpu.CompilerParams(vmem_limit_bytes=60 << 20),
    )(grad_rows, grad_scale[None, :], route_probs.T, expert_ids.T)


def spread_rows(me, hidden_ref, label_refs, out_ref, table_ref, rows_ref):
    experts, sources, capacity, units = hidden_ref.shape
    tok = label_refs[0].shape[0]
    slot = lax.broadcasted_iota(jnp.int32, (capacity, tok), 0).astype(jnp.float32)
    for q in range(sources):
        src = me ^ q
        table_ref[...] = label_refs[q][...].astype(jnp.float32).T
        for j in range(experts):
            line = lambda part: table_ref[pl.ds(part * EXPERTS + me * experts + j, 1), :]
            pos = line(0)
            coef = line(1) + line(2) + line(3)
            pick = jnp.where(slot == pos, 1.0, 0.0).astype(jnp.bfloat16)
            rows = lax.dot_general(
                hidden_ref[j, src],
                pick,
                (((0,), (0,)), ((), ())),
                preferred_element_type=jnp.float32,
            )
            rows_ref[pl.ds(j, units, stride=experts), :] = rows * coef
        out_ref[:, q * tok : (q + 1) * tok] = rows_ref[...].astype(out_ref.dtype)


def last_block(label, tok):
    last = label.shape[1] // tok - 1
    return pl.BlockSpec((tok, tok), lambda i, w: (0, last))


def spread_call(body, where, hiddens, unit_blocks, labels, n_out):
    experts, sources, capacity = hiddens[0].shape[:3]
    tok = labels[0].shape[0]
    units = hiddens[0].shape[3] // unit_blocks
    out = jax.ShapeDtypeStruct((units * experts, sources * tok), jnp.bfloat16)
    out_spec = pl.BlockSpec(out.shape, lambda i, w: (0, 0))
    return pl.pallas_call(
        body,
        grid_spec=pltpu.PrefetchScalarGridSpec(
            num_scalar_prefetch=1,
            grid=(1,),
            in_specs=[
                pl.BlockSpec(
                    (experts, sources, capacity, units),
                    (lambda i, w: (0, 0, 0, w[1])) if unit_blocks > 1 else (lambda i, w: (0, 0, 0, 0)),
                )
                for _ in hiddens
            ]
            + [last_block(label, tok) for label in labels],
            out_specs=[out_spec] * n_out,
            scratch_shapes=[
                pltpu.VMEM((tok, tok), jnp.float32),
                pltpu.VMEM((units * experts, tok), jnp.float32),
            ],
        ),
        out_shape=[out] * n_out,
        compiler_params=pltpu.CompilerParams(vmem_limit_bytes=16 << 20),
        cost_estimate=pl.CostEstimate(
            flops=4 * n_out * sources * tok * units * experts * capacity,
            bytes_accessed=n_out * (hiddens[0].size * 2 + out.size * 2),
            transcendentals=0,
        ),
    )(where, *hiddens, *labels)


def spread(where, hidden, unit_blocks, labels):
    def body(where_ref, hidden_ref, *refs):
        *label_refs, out_ref, table_ref, rows_ref = refs
        spread_rows(where_ref[0], hidden_ref, label_refs, out_ref, table_ref, rows_ref)

    return spread_call(body, where, [hidden], unit_blocks, labels, 1)[0]


def spread_far(where, hidden_ends, hidden_inner, labels):
    def body(where_ref, ends_ref, inner_ref, *refs):
        *label_refs, out_ref, table_ref, rows_ref = refs

        @pl.when(where_ref[2] == 1)
        def _():
            spread_rows(where_ref[0], ends_ref, label_refs, out_ref, table_ref, rows_ref)

        @pl.when(where_ref[2] == 0)
        def _():
            spread_rows(where_ref[0], inner_ref, label_refs, out_ref, table_ref, rows_ref)

    return spread_call(body, where, [hidden_ends, hidden_inner], 1, labels, 1)[0]


def product(spreads, rows, width, acc=None, last=False, experts=4, tile=512, cost=1):
    n_tok = rows[0].shape[0]
    m = spreads[0].shape[0]
    k = sum(s.shape[1] for s in spreads)

    def body(*refs):
        refs = list(refs)
        lhs = [refs.pop(0) for _ in spreads]
        held = [refs.pop(0) for _ in rows]
        before = refs.pop(0) if acc is not None else None
        out = refs.pop(0)
        right = jnp.concatenate([r[...] for r in held], axis=0)
        left = jnp.concatenate([r[...] for r in lhs], axis=1) if len(lhs) > 1 else lhs[0][...]
        total = jnp.dot(left, right, preferred_element_type=jnp.float32)
        if before is not None:
            total = total + before[...].astype(jnp.float32)
        if last:
            out[...] = total.reshape(m // experts, experts, tile).astype(out.dtype)
        else:
            out[...] = total.astype(out.dtype)

    in_specs = [
        pl.BlockSpec(s.shape, lambda i: (0, 0), pipeline_mode=pl.Buffered(1)) for s in spreads
    ]
    in_specs += [pl.BlockSpec((n_tok, tile), lambda i: (0, i)) for _ in rows]
    args = [*spreads, *rows]
    if acc is not None:
        in_specs.append(pl.BlockSpec((m, tile), lambda i: (0, i)))
        args.append(acc)
    if last:
        out_shape = jax.ShapeDtypeStruct((m // experts, experts, width), jnp.bfloat16)
        out_spec = pl.BlockSpec((m // experts, experts, tile), lambda i: (0, 0, i))
    else:
        out_shape = jax.ShapeDtypeStruct((m, width), ACC)
        out_spec = pl.BlockSpec((m, tile), lambda i: (0, i))
    return pl.pallas_call(
        body,
        grid=(width // tile,),
        in_specs=in_specs,
        out_specs=out_spec,
        out_shape=out_shape,
        compiler_params=pltpu.CompilerParams(vmem_limit_bytes=20 << 20),
        cost_estimate=pl.CostEstimate(
            flops=cost * 2 * m * k * width,
            bytes_accessed=cost * (m * width * 4 + k * width * 2),
            transcendentals=0,
        ),
    )(*args)


def gathered_shards(grad_rows, grad_scale, route_probs, expert_ids, saved_hidden):
    tok, width = grad_rows.shape
    top_count = expert_ids.shape[1]
    n_expert = lax.axis_size("expert")
    n_replica = lax.axis_size("replica")
    per_device = EXPERTS // n_expert
    hidden = saved_hidden[0]
    units = hidden.shape[3] // n_replica
    scale_norm = 1.0 / math.sqrt(n_replica * n_expert * tok * top_count / EXPERTS)
    e = lax.axis_index("expert")
    z = lax.axis_index("replica")
    both = ("expert", "replica")

    def send(name, array, expert_to, moves):
        pairs = [
            (a * n_replica + i, expert_to(a) * n_replica + j)
            for a in range(n_expert)
            for i, j in moves
        ]
        with jax.named_scope(name):
            return lax.ppermute(array, both, pairs)

    stay = [(i, i) for i in range(4)]
    near = [(0, 1), (1, 0), (2, 3), (3, 2)]
    middle = [(1, 2), (2, 1)]
    outward = [(1, 0), (2, 3)]
    outer = [(0, 3), (3, 0)]
    cross_in = [(2, 0), (1, 3)]
    cross_out = [(0, 2), (3, 1)]
    same = lambda a: a
    core = lambda a: a ^ 1
    side = lambda a: a ^ 2
    inner = (z == 1) | (z == 2)

    def units_of(replica):
        return lax.dynamic_slice_in_dim(hidden, replica * units, units, 3)

    own = labelled(grad_rows, grad_scale, route_probs, expert_ids, scale_norm)

    tie = lax.optimization_barrier
    h_near, h_cross, h_flip = (units_of(z ^ i) for i in range(1, 4))
    where = jnp.stack([e, z, jnp.where(inner, 0, 1)]).astype(jnp.int32)

    c_own = send("c_own", own, core, stay)
    mid_a = send("mid_a", own, same, middle)
    x_own = send("x_own", own, side, stay)
    pair = send("pair", own, same, near)
    own, c_own, mid_a, x_own, pair, where, h_near, h_cross, h_flip = tie(
        (own, c_own, mid_a, x_own, pair, where, h_near, h_cross, h_flip)
    )

    end_a = send("end_a", mid_a, same, outward)
    mid_b = send("mid_b", pair, same, middle)
    x_pair = send("x_pair", pair, side, stay)
    g_near = send("g_near", h_near, same, near)
    g_inner = send("g_inner", h_flip, same, middle)
    c_xown = send("c_xown", x_own, core, stay)
    far_a = jnp.where(inner, mid_a, end_a)
    x_pair, g_near, g_inner, c_xown, far_a, mid_b, own, c_own, x_own, pair, h_cross, h_flip = tie(
        (x_pair, g_near, g_inner, c_xown, far_a, mid_b, own, c_own, x_own, pair, h_cross, h_flip)
    )

    end_b = send("end_b", mid_b, same, outward)
    g_out = send("g_out", h_cross, same, cross_out)
    x_far_a = send("x_far_a", far_a, side, stay)
    c_xpair = send("c_xpair", x_pair, core, stay)
    c_pair = send("c_pair", pair, core, stay)
    l_xfar_a = x_far_a[:, width:]
    s_own = spread(where, hidden, n_replica, [own, c_own, x_own, c_xown])
    acc = product([s_own], [own, c_own, x_own, c_xown], width)
    far_b = jnp.where(inner, mid_b, end_b)
    far_b, x_far_a, l_xfar_a, g_out, c_xpair, c_pair, acc, pair, x_pair, far_a, h_cross, h_flip = tie(
        (far_b, x_far_a, l_xfar_a, g_out, c_xpair, c_pair, acc, pair, x_pair, far_a, h_cross, h_flip)
    )

    x_far_b = send("x_far_b", far_b, side, stay)
    g_in = send("g_in", h_cross, same, cross_in)
    c_far_a = send("c_far_a", far_a, core, stay)
    c_xfar_a = send("c_xfar_a", x_far_a, core, stay)
    rows_near = [pair, c_pair, x_pair, c_xpair]
    s_near = spread(where, g_near, 1, rows_near)
    acc = product([s_near], rows_near, width, acc, cost=4)
    g_in, acc, h_flip, far_b = tie(
        (g_in, acc, h_flip, far_b)
    )

    g_outer = send("g_outer", h_flip, same, outer)
    c_far_b = send("c_far_b", far_b, core, stay)
    s_a = spread_far(where, g_in, g_inner, [far_a, c_far_a, l_xfar_a, c_xfar_a])
    x_far_b, acc = tie(
        (x_far_b, acc)
    )
    c_xfar_b = send("c_xfar_b", x_far_b, core, stay)
    acc = product([s_a], [far_a, c_far_a, x_far_a, c_xfar_a], width, acc, cost=4)
    g_outer, c_xfar_b, c_far_b, acc, far_b = tie(
        (g_outer, c_xfar_b, c_far_b, acc, far_b)
    )

    rows_b = [far_b, c_far_b, x_far_b, c_xfar_b]
    s_b = spread_far(where, g_outer, g_out, rows_b)
    return product([s_b], rows_b, width, acc, last=True, experts=per_device)


def solution(mesh):
    placed = (
        P(("groups", "expert", "replica"), None),
        P(("groups", "expert", "replica")),
        P(("groups", "expert", "replica"), None),
        P(("groups", "expert", "replica"), None),
        P(("groups", "replica"), "expert", None, None, None),
    )
    small = mesh.shape["expert"] == 4 and mesh.shape["replica"] == 4
    return jax.shard_map(
        gathered_shards if small else summed_shards,
        mesh=mesh,
        in_specs=placed,
        out_specs=P(("groups", "replica"), "expert", None),
        check_vma=False,
    )
```

```python
import functools
import math

import jax
import jax.numpy as jnp
from jax import lax
from jax.experimental import pallas as pl
from jax.experimental.pallas import tpu as pltpu
from jax.sharding import PartitionSpec as P

EXPERTS = 16
ACC = jnp.bfloat16


def slot_positions(expert_ids):
    flat_ids = expert_ids.reshape(-1)
    onehot = (flat_ids[:, None] == jnp.arange(EXPERTS, dtype=jnp.int32)[None, :]).astype(jnp.int32)
    running = jnp.cumsum(onehot, axis=0)
    return (flat_ids, jnp.sum(onehot * running, axis=1) - 1)


def summed_shards(grad_rows, grad_scale, route_probs, expert_ids, saved_hidden):
    tok_rows, row_width = grad_rows.shape
    top_count = expert_ids.shape[1]
    n_expert = lax.axis_size("expert")
    n_replica = lax.axis_size("replica")
    per_device = EXPERTS // n_expert
    hidden = saved_hidden[0]
    capacity = hidden.shape[2]
    hidden_units = hidden.shape[3]
    scale_norm = 1.0 / math.sqrt(n_replica * n_expert * tok_rows * top_count / EXPERTS)
    flat_ids, position = slot_positions(expert_ids)
    pair_coef = grad_scale[:, None] * route_probs
    gathered_ids, gathered_pos = (
        lax.all_gather(expert_ids, "expert", axis=0, tiled=True),
        lax.all_gather(position.reshape(tok_rows, top_count), "expert", axis=0, tiled=True),
    )
    gathered_coef = lax.all_gather(pair_coef, "expert", axis=0, tiled=True)
    first_expert = lax.axis_index("expert") * per_device
    local_ids = first_expert + jnp.arange(per_device, dtype=jnp.int32)
    hidden_flat = hidden.reshape(per_device, n_expert * capacity, hidden_units)
    token_piece = lax.all_gather(grad_rows, "expert", axis=0, tiled=True)
    row_count = token_piece.shape[0]
    source = jnp.arange(row_count, dtype=jnp.int32) // tok_rows
    matches = gathered_ids[None, :, :] == local_ids[:, None, None]
    row_coef = jnp.sum(jnp.where(matches, gathered_coef[None], 0.0), axis=2)
    row_index = jnp.sum(
        jnp.where(matches, source[None, :, None] * capacity + gathered_pos[None], 0), axis=2
    )
    chosen = jax.vmap(lambda hidden_table, row_pick: jnp.take(hidden_table, row_pick, axis=0))(
        hidden_flat, row_index
    )
    scaled = (row_coef[:, :, None] * token_piece[None]).astype(jnp.bfloat16)
    summed = jnp.einsum("lif,lid->fld", chosen, scaled, preferred_element_type=jnp.float32)
    return lax.psum_scatter(
        (summed * scale_norm).astype(jnp.bfloat16), "replica", scatter_dimension=0, tiled=True
    )


def label_kernel(scale_norm, rows_ref, scale_ref, probs_ref, ids_ref, out_ref):
    tok, width = rows_ref.shape
    out_ref[:, :width] = rows_ref[...]
    coef = probs_ref[...] * scale_ref[...] * scale_norm
    ids = ids_ref[...]
    masks, coefs = [], []
    for j in range(EXPERTS):
        named = ids == j
        masks.append(jnp.sum(jnp.where(named, 1.0, 0.0), axis=0, keepdims=True))
        coefs.append(jnp.sum(jnp.where(named, coef, 0.0), axis=0, keepdims=True))
    mask = jnp.concatenate(masks, axis=0)
    coef = jnp.concatenate(coefs, axis=0)
    row = lax.broadcasted_iota(jnp.int32, (tok, tok), 0)
    col = lax.broadcasted_iota(jnp.int32, (tok, tok), 1)
    before = jnp.where(row < col, 1.0, 0.0).astype(jnp.bfloat16)
    place = jnp.dot(mask.astype(jnp.bfloat16), before, preferred_element_type=jnp.float32)
    place = jnp.where(mask > 0.0, place, -1.0)
    high = coef.astype(jnp.bfloat16).astype(jnp.float32)
    mid = (coef - high).astype(jnp.bfloat16).astype(jnp.float32)
    low = coef - high - mid
    rest = jnp.zeros((tok - 4 * EXPERTS, tok), jnp.float32)
    labels = jnp.concatenate([place, high, mid, low, rest], axis=0)
    out_ref[:, width:] = labels.T.astype(out_ref.dtype)


def labelled(grad_rows, grad_scale, route_probs, expert_ids, scale_norm):
    tok, width = grad_rows.shape
    return pl.pallas_call(
        functools.partial(label_kernel, scale_norm),
        out_shape=jax.ShapeDtypeStruct((tok, width + tok), grad_rows.dtype),
        compiler_params=pltpu.CompilerParams(vmem_limit_bytes=60 << 20),
    )(grad_rows, grad_scale[None, :], route_probs.T, expert_ids.T)


def spread_rows(me, hidden_ref, label_refs, out_ref, table_ref, rows_ref):
    experts, sources, capacity, units = hidden_ref.shape
    tok = label_refs[0].shape[0]
    slot = lax.broadcasted_iota(jnp.int32, (capacity, tok), 0).astype(jnp.float32)
    for q in range(sources):
        src = me ^ q
        table_ref[...] = label_refs[q][...].astype(jnp.float32).T
        for j in range(experts):
            line = lambda part: table_ref[pl.ds(part * EXPERTS + me * experts + j, 1), :]
            pos = line(0)
            coef = line(1) + line(2) + line(3)
            pick = jnp.where(slot == pos, 1.0, 0.0).astype(jnp.bfloat16)
            rows = lax.dot_general(
                hidden_ref[j, src],
                pick,
                (((0,), (0,)), ((), ())),
                preferred_element_type=jnp.float32,
            )
            rows_ref[pl.ds(j, units, stride=experts), :] = rows * coef
        out_ref[:, q * tok : (q + 1) * tok] = rows_ref[...].astype(out_ref.dtype)


def last_block(label, tok):
    last = label.shape[1] // tok - 1
    return pl.BlockSpec((tok, tok), lambda i, w: (0, last))


def spread_call(body, where, hiddens, unit_blocks, labels, n_out):
    experts, sources, capacity = hiddens[0].shape[:3]
    tok = labels[0].shape[0]
    units = hiddens[0].shape[3] // unit_blocks
    out = jax.ShapeDtypeStruct((units * experts, sources * tok), jnp.bfloat16)
    out_spec = pl.BlockSpec(out.shape, lambda i, w: (0, 0))
    return pl.pallas_call(
        body,
        grid_spec=pltpu.PrefetchScalarGridSpec(
            num_scalar_prefetch=1,
            grid=(1,),
            in_specs=[
                pl.BlockSpec(
                    (experts, sources, capacity, units),
                    (lambda i, w: (0, 0, 0, w[1])) if unit_blocks > 1 else (lambda i, w: (0, 0, 0, 0)),
                )
                for _ in hiddens
            ]
            + [last_block(label, tok) for label in labels],
            out_specs=[out_spec] * n_out,
            scratch_shapes=[
                pltpu.VMEM((tok, tok), jnp.float32),
                pltpu.VMEM((units * experts, tok), jnp.float32),
            ],
        ),
        out_shape=[out] * n_out,
        compiler_params=pltpu.CompilerParams(vmem_limit_bytes=16 << 20),
        cost_estimate=pl.CostEstimate(
            flops=4 * n_out * sources * tok * units * experts * capacity,
            bytes_accessed=n_out * (hiddens[0].size * 2 + out.size * 2),
            transcendentals=0,
        ),
    )(where, *hiddens, *labels)


def spread(where, hidden, unit_blocks, labels):
    def body(where_ref, hidden_ref, *refs):
        *label_refs, out_ref, table_ref, rows_ref = refs
        spread_rows(where_ref[0], hidden_ref, label_refs, out_ref, table_ref, rows_ref)

    return spread_call(body, where, [hidden], unit_blocks, labels, 1)[0]


def spread_far(where, hidden_ends, hidden_inner, labels):
    def body(where_ref, ends_ref, inner_ref, *refs):
        *label_refs, out_ref, table_ref, rows_ref = refs

        @pl.when(where_ref[2] == 1)
        def _():
            spread_rows(where_ref[0], ends_ref, label_refs, out_ref, table_ref, rows_ref)

        @pl.when(where_ref[2] == 0)
        def _():
            spread_rows(where_ref[0], inner_ref, label_refs, out_ref, table_ref, rows_ref)

    return spread_call(body, where, [hidden_ends, hidden_inner], 1, labels, 1)[0]


def product(spreads, rows, width, acc=None, last=False, experts=4, tile=896, cost=1):
    n_tok = rows[0].shape[0]
    m = spreads[0].shape[0]
    k = sum(s.shape[1] for s in spreads)

    def body(*refs):
        refs = list(refs)
        lhs = [refs.pop(0) for _ in spreads]
        held = [refs.pop(0) for _ in rows]
        before = refs.pop(0) if acc is not None else None
        out = refs.pop(0)
        right = jnp.concatenate([r[...] for r in held], axis=0)
        left = jnp.concatenate([r[...] for r in lhs], axis=1) if len(lhs) > 1 else lhs[0][...]
        total = jnp.dot(left, right, preferred_element_type=jnp.float32)
        if before is not None:
            total = total + before[...].astype(jnp.float32)
        if last:
            out[...] = total.reshape(m // experts, experts, tile).astype(out.dtype)
        else:
            out[...] = total.astype(out.dtype)

    in_specs = [
        pl.BlockSpec(s.shape, lambda i: (0, 0), pipeline_mode=pl.Buffered(1)) for s in spreads
    ]
    in_specs += [pl.BlockSpec((n_tok, tile), lambda i: (0, i)) for _ in rows]
    args = [*spreads, *rows]
    if acc is not None:
        in_specs.append(pl.BlockSpec((m, tile), lambda i: (0, i)))
        args.append(acc)
    if last:
        out_shape = jax.ShapeDtypeStruct((m // experts, experts, width), jnp.bfloat16)
        out_spec = pl.BlockSpec((m // experts, experts, tile), lambda i: (0, 0, i))
    else:
        out_shape = jax.ShapeDtypeStruct((m, width), ACC)
        out_spec = pl.BlockSpec((m, tile), lambda i: (0, i))
    return pl.pallas_call(
        body,
        grid=(width // tile,),
        in_specs=in_specs,
        out_specs=out_spec,
        out_shape=out_shape,
        compiler_params=pltpu.CompilerParams(vmem_limit_bytes=20 << 20),
        cost_estimate=pl.CostEstimate(
            flops=cost * 2 * m * k * width,
            bytes_accessed=cost * (m * width * 4 + k * width * 2),
            transcendentals=0,
        ),
    )(*args)


def gathered_shards(grad_rows, grad_scale, route_probs, expert_ids, saved_hidden):
    tok, width = grad_rows.shape
    top_count = expert_ids.shape[1]
    n_expert = lax.axis_size("expert")
    n_replica = lax.axis_size("replica")
    per_device = EXPERTS // n_expert
    hidden = saved_hidden[0]
    units = hidden.shape[3] // n_replica
    scale_norm = 1.0 / math.sqrt(n_replica * n_expert * tok * top_count / EXPERTS)
    e = lax.axis_index("expert")
    z = lax.axis_index("replica")
    both = ("expert", "replica")

    def send(name, array, expert_to, moves):
        pairs = [
            (a * n_replica + i, expert_to(a) * n_replica + j)
            for a in range(n_expert)
            for i, j in moves
        ]
        with jax.named_scope(name):
            return lax.ppermute(array, both, pairs)

    stay = [(i, i) for i in range(4)]
    near = [(0, 1), (1, 0), (2, 3), (3, 2)]
    middle = [(1, 2), (2, 1)]
    outward = [(1, 0), (2, 3)]
    outer = [(0, 3), (3, 0)]
    cross_in = [(2, 0), (1, 3)]
    cross_out = [(0, 2), (3, 1)]
    same = lambda a: a
    core = lambda a: a ^ 1
    side = lambda a: a ^ 2
    inner = (z == 1) | (z == 2)

    def units_of(replica):
        return lax.dynamic_slice_in_dim(hidden, replica * units, units, 3)

    own = labelled(grad_rows, grad_scale, route_probs, expert_ids, scale_norm)

    tie = lax.optimization_barrier
    h_near, h_cross, h_flip = (units_of(z ^ i) for i in range(1, 4))
    where = jnp.stack([e, z, jnp.where(inner, 0, 1)]).astype(jnp.int32)

    c_own = send("c_own", own, core, stay)
    mid_a = send("mid_a", own, same, middle)
    x_own = send("x_own", own, side, stay)
    pair = send("pair", own, same, near)
    own, c_own, mid_a, x_own, pair, where, h_near, h_cross, h_flip = tie(
        (own, c_own, mid_a, x_own, pair, where, h_near, h_cross, h_flip)
    )

    end_a = send("end_a", mid_a, same, outward)
    mid_b = send("mid_b", pair, same, middle)
    x_pair = send("x_pair", pair, side, stay)
    g_near = send("g_near", h_near, same, near)
    g_inner = send("g_inner", h_flip, same, middle)
    c_xown = send("c_xown", x_own, core, stay)
    far_a = jnp.where(inner, mid_a, end_a)
    x_pair, g_near, g_inner, c_xown, far_a, mid_b, own, c_own, x_own, pair, h_cross, h_flip = tie(
        (x_pair, g_near, g_inner, c_xown, far_a, mid_b, own, c_own, x_own, pair, h_cross, h_flip)
    )

    end_b = send("end_b", mid_b, same, outward)
    g_out = send("g_out", h_cross, same, cross_out)
    x_far_a = send("x_far_a", far_a, side, stay)
    c_xpair = send("c_xpair", x_pair, core, stay)
    c_pair = send("c_pair", pair, core, stay)
    l_xfar_a = x_far_a[:, width:]
    s_own = spread(where, hidden, n_replica, [own, c_own, x_own, c_xown])
    acc = product([s_own], [own, c_own, x_own, c_xown], width)
    far_b = jnp.where(inner, mid_b, end_b)
    far_b, x_far_a, l_xfar_a, g_out, c_xpair, c_pair, acc, pair, x_pair, far_a, h_cross, h_flip = tie(
        (far_b, x_far_a, l_xfar_a, g_out, c_xpair, c_pair, acc, pair, x_pair, far_a, h_cross, h_flip)
    )

    x_far_b = send("x_far_b", far_b, side, stay)
    g_in = send("g_in", h_cross, same, cross_in)
    c_far_a = send("c_far_a", far_a, core, stay)
    c_xfar_a = send("c_xfar_a", x_far_a, core, stay)
    rows_near = [pair, c_pair, x_pair, c_xpair]
    s_near = spread(where, g_near, 1, rows_near)
    acc = product([s_near], rows_near, width, acc, cost=4)
    g_in, acc, h_flip, far_b = tie(
        (g_in, acc, h_flip, far_b)
    )

    g_outer = send("g_outer", h_flip, same, outer)
    c_far_b = send("c_far_b", far_b, core, stay)
    s_a = spread_far(where, g_in, g_inner, [far_a, c_far_a, l_xfar_a, c_xfar_a])
    x_far_b, acc = tie(
        (x_far_b, acc)
    )
    c_xfar_b = send("c_xfar_b", x_far_b, core, stay)
    acc = product([s_a], [far_a, c_far_a, x_far_a, c_xfar_a], width, acc, cost=4)
    g_outer, c_xfar_b, c_far_b, acc, far_b = tie(
        (g_outer, c_xfar_b, c_far_b, acc, far_b)
    )

    rows_b = [far_b, c_far_b, x_far_b, c_xfar_b]
    s_b = spread_far(where, g_outer, g_out, rows_b)
    return product([s_b], rows_b, width, acc, last=True, experts=per_device)


def solution(mesh):
    placed = (
        P(("groups", "expert", "replica"), None),
        P(("groups", "expert", "replica")),
        P(("groups", "expert", "replica"), None),
        P(("groups", "expert", "replica"), None),
        P(("groups", "replica"), "expert", None, None, None),
    )
    small = mesh.shape["expert"] == 4 and mesh.shape["replica"] == 4
    return jax.shard_map(
        gathered_shards if small else summed_shards,
        mesh=mesh,
        in_specs=placed,
        out_specs=P(("groups", "replica"), "expert", None),
        check_vma=False,
    )
```
